32 devices in a mesh: member: 8 (over z, x), region: 4 (over y, core).
Axes of the slice: x: 2, y: 2, z: 4, core: 2. Of those that a mesh axis runs over, the one named last changes fastest.
Arguments:
- ensemble: bfloat16 [1024, 4, 8, 512], P('member', 'region'), may hold values from -6 to 6
- obs_store: bfloat16 [4, 8, 5, 128, 1024], P('region', 'member'), may hold values from -4 to 4
- block_ids: int32 [4, 8, 3], P('region', 'member'), may hold values from 0 to 4, as said below
- block_src: int32 [4, 8, 3], P('region', 'member'), may hold values from 0 to 2, as said below
- block_count: int32 [4, 8], P('region', 'member'), may hold values from 1 to 3, as said below
Outputs:
- analysis: bfloat16 [1024, 4, 8, 512], P('member', 'region')
The draws below stay inside these ranges and needn't reach their ends.
Inputs may be any that keep to these rules, and one draw needn't show every extreme that they name: `block_ids`: within one patch's list the first 3 entries are distinct store indices. `block_src`: region 0 never names the region below and region 4 - 1 never names the region above. `block_count`: every region has a patch with 3 blocks.
All inputs are finite; a program needn't handle non-finite values.
Results may differ from the reference program's by a relative error of at most 0.0021.
Values may be sent and summed in bfloat16 or wider, within the bound.
No kernel may reach another device: no remote copies, remote signals or barrier semaphores. Data moves between devices by JAX's collectives and lax.ppermute only.
A program may use at most 64 MiB of HBM per device.

```python
import jax
import jax.numpy as jnp
from jax import lax

K = 1024
V = 512
ROWS = 128
OBS_DEV = 5
MAXB = 3
REGIONS = 4
PATCHES = 8


def draw_obs_store(key, part):
    shape = (REGIONS, PATCHES, OBS_DEV, ROWS, K)
    main_key = jax.random.fold_in(key, 101)
    values = 0.6 * jax.random.normal(main_key, shape, jnp.float32)
    return jnp.clip(values, -4.0, 4.0).astype(jnp.bfloat16)


def draw_block_ids(key, part):
    scores = jax.random.randint(key, (REGIONS, PATCHES, OBS_DEV), 0, 1 << 20)
    scores = scores * OBS_DEV + jnp.arange(OBS_DEV, dtype=jnp.int32)[None, None, :]
    order_ids = jnp.argsort(scores, axis=-1, stable=True)
    return order_ids[:, :, :MAXB].astype(jnp.int32)


def draw_block_src(key, part):
    codes = jax.random.randint(key, (REGIONS, PATCHES, MAXB), 0, 3)
    region_idx = jnp.arange(REGIONS, dtype=jnp.int32)[:, None, None]
    codes = jnp.where((region_idx == 0) & (codes == 0), 1, codes)
    codes = jnp.where((region_idx == REGIONS - 1) & (codes == 2), 1, codes)
    return codes.astype(jnp.int32)


def draw_block_count(key, part):
    first_key = jax.random.fold_in(key, 11)
    second_key = jax.random.fold_in(key, 23)
    counts = jax.random.randint(first_key, (REGIONS, PATCHES), 1, MAXB + 1)
    chosen = jax.random.randint(second_key, (REGIONS,), 0, PATCHES)
    patch_idx = jnp.arange(PATCHES, dtype=jnp.int32)[None, :]
    counts = jnp.where(patch_idx == chosen[:, None], MAXB, counts)
    return counts.astype(jnp.int32)


def block_scale(stream_key, shape, split, least, high):
    def one(position, parts):
        draws = jax.random.uniform(jax.random.fold_in(jax.random.fold_in(stream_key, 6), position), (parts,), jnp.float32, least / len(split), high / len(split))
        return jnp.repeat(jnp.exp(draws), shape[position] // parts).reshape((-1,) + (1,) * (len(shape) - position - 1))

    level = one(*split[0])
    for cut in split[1:]:
        level = level * one(*cut)
    return level


def scatter_about(key, extent, scale, reach, cuts=(), kind=jnp.bfloat16):
    gain = block_scale(key, extent, cuts, -0.22, 0.18) if cuts else 1.0
    values = jax.random.normal(key, extent, jnp.float32) * scale * gain
    return jnp.minimum(jnp.maximum(values, -reach), reach).astype(kind)


def setup_inputs(seed: int = 0) -> dict:
    key_list = jax.random.split(jax.random.key(seed), 6)
    return {
        "ensemble": scatter_about(key_list[0], (K, REGIONS, PATCHES, V), 1.0, 6.0, ((0, 8), (1, 4))),
        "obs_store": draw_obs_store(jax.random.fold_in(key_list[5], 71), 0),
        "block_ids": draw_block_ids(jax.random.fold_in(key_list[5], 71), 0),
        "block_src": draw_block_src(jax.random.fold_in(key_list[5], 71), 0),
        "block_count": draw_block_count(jax.random.fold_in(key_list[5], 71), 0),
    }


def reference(ensemble, obs_store, block_ids, block_src, block_count):
    regions = block_count.shape[0]
    patches = block_count.shape[1]
    highest = lax.Precision.HIGHEST

    def one_patch(index):
        region = index // patches
        patch = index % patches
        slot_ids = block_ids[region, patch]
        slot_src = block_src[region, patch]
        used = block_count[region, patch]
        source = jnp.clip(region + slot_src - 1, 0, regions - 1)
        blocks = obs_store[source, patch, slot_ids]
        live_slots = jnp.arange(MAXB, dtype=jnp.int32) < used
        blocks = jnp.where(live_slots[:, None, None], blocks, jnp.zeros((), blocks.dtype))
        stacked = blocks.astype(jnp.float32).reshape(-1, blocks.shape[2])
        gram_full = jnp.dot(stacked.T, stacked, precision=highest) / (2.0 * K)
        gram_matrix = lax.optimization_barrier(gram_full.astype(jnp.bfloat16)).astype(jnp.float32)
        members = ensemble[:, region, patch, :].astype(jnp.float32)
        first_term = jnp.dot(gram_matrix, members, precision=highest).astype(jnp.bfloat16)
        first_term = lax.optimization_barrier(first_term).astype(jnp.float32)
        second_term = jnp.dot(gram_matrix, first_term, precision=highest)
        return (members - first_term + second_term).astype(jnp.bfloat16)

    result = lax.map(one_patch, jnp.arange(regions * patches, dtype=jnp.int32))
    result = result.reshape(regions, patches, result.shape[1], result.shape[2])
    return jnp.transpose(result, (2, 0, 1, 3))
```

```python
import functools

import jax
import jax.numpy as jnp
from jax import lax
from jax.experimental import pallas as pl
from jax.experimental.pallas import tpu as pltpu
from jax.sharding import PartitionSpec as P

CHUNKS = 2
LIMIT = 40 * 1024 * 1024


def rows_per_group(rows, patches):
    return min(rows, max(16, 256 // patches))


def shuffle_matrix(height, outer, inner):
    row = lax.broadcasted_iota(jnp.int32, (height, height), 0)
    column = lax.broadcasted_iota(jnp.int32, (height, height), 1)
    source = lax.rem(row, inner) * outer + lax.div(row, inner)
    return jnp.where(column == source, 1.0, 0.0).astype(jnp.bfloat16)


def split_kernel(patches, members_ref, *out_refs):
    rows = out_refs[0].shape[1]
    width = out_refs[0].shape[2]
    group = rows_per_group(rows, patches)
    height = group * patches
    shuffle = shuffle_matrix(height, patches, group)
    for step in range(rows // group):
        block = members_ref[step * height : (step + 1) * height, :]
        moved = jnp.dot(shuffle, block, preferred_element_type=jnp.float32)
        moved = moved.astype(jnp.bfloat16).reshape(patches, group, block.shape[1])
        for chunk, out_ref in enumerate(out_refs):
            out_ref[:, step * group : (step + 1) * group, :] = moved[
                :, :, chunk * width : (chunk + 1) * width
            ]


def merge_kernel(patches, *refs):
    chunk_refs, out_ref = refs[:-1], refs[-1]
    rows = chunk_refs[0].shape[1]
    width = chunk_refs[0].shape[2]
    group = rows_per_group(rows, patches)
    height = group * patches
    shuffle = shuffle_matrix(height, group, patches)
    for step in range(rows // group):
        for chunk, chunk_ref in enumerate(chunk_refs):
            block = chunk_ref[:, step * group : (step + 1) * group, :].reshape(height, width)
            moved = jnp.dot(shuffle, block, preferred_element_type=jnp.float32)
            out_ref[
                step * height : (step + 1) * height, chunk * width : (chunk + 1) * width
            ] = moved.astype(jnp.bfloat16)


def gram_kernel(scale, ids_ref, src_ref, count_ref, below, own, above, gram_ref, stacked, sem):
    slots = ids_ref.shape[0]
    rows = own.shape[1]
    for slot in range(slots):
        live = slot < count_ref[0]
        target = stacked.at[pl.ds(slot * rows, rows), :]
        for code, store in enumerate((below, own, above)):

            @pl.when(live & (src_ref[slot] == code))
            def _():
                pltpu.make_async_copy(store.at[ids_ref[slot]], target, sem.at[slot]).start()

        @pl.when(jnp.logical_not(live))
        def _():
            target[...] = jnp.zeros(target.shape, target.dtype)

    for slot in range(slots):

        @pl.when(slot < count_ref[0])
        def _():
            target = stacked.at[pl.ds(slot * rows, rows), :]
            pltpu.make_async_copy(own.at[0], target, sem.at[slot]).wait()

    size = gram_ref.shape[0]
    part = min(size, 256)
    for step in range(size // part):
        block = lax.dot_general(
            stacked[:, step * part : (step + 1) * part],
            stacked[...],
            (((0,), (0,)), ((), ())),
            preferred_element_type=jnp.float32,
        )
        gram_ref[step * part : (step + 1) * part, :] = (block * scale).astype(jnp.bfloat16)


def transform_kernel(gram_ref, members_ref, out_ref, first):
    size = gram_ref.shape[0]
    part = min(size, 256)
    for step in range(size // part):
        here = slice(step * part, (step + 1) * part)
        first[here, :] = jnp.dot(
            gram_ref[here, :], members_ref[...], preferred_element_type=jnp.float32
        ).astype(jnp.bfloat16)
    for step in range(size // part):
        here = slice(step * part, (step + 1) * part)
        second = jnp.dot(gram_ref[here, :], first[...], preferred_element_type=jnp.float32)
        fresh = members_ref[here, :].astype(jnp.float32) - first[here, :].astype(jnp.float32)
        out_ref[here, :] = (fresh + second).astype(jnp.bfloat16)


def vmem():
    return pl.BlockSpec(memory_space=pltpu.VMEM)


def params():
    return pltpu.CompilerParams(vmem_limit_bytes=LIMIT)


def cost(flops, nbytes):
    return pl.CostEstimate(flops=flops, bytes_accessed=nbytes, transcendentals=0)


def neighbours(store):
    count = lax.axis_size("region")
    up = [(i, i + 1) for i in range(count - 1)]
    down = [(i + 1, i) for i in range(count - 1)]
    return lax.ppermute(store, "region", up), lax.ppermute(store, "region", down)


def shards(ensemble, obs_store, block_ids, block_src, block_count):
    rows, _, patches, values = ensemble.shape
    store = obs_store.reshape(obs_store.shape[2:])
    size = store.shape[2]
    slots = block_ids.shape[2]
    width = values // CHUNKS
    below, above = neighbours(store)

    pieces = pl.pallas_call(
        functools.partial(split_kernel, patches),
        out_shape=[jax.ShapeDtypeStruct((patches, rows, width), jnp.bfloat16)] * CHUNKS,
        in_specs=[vmem()],
        out_specs=[vmem()] * CHUNKS,
        compiler_params=params(),
        cost_estimate=cost(2 * 256 * rows * patches * values, 4 * rows * patches * values),
        name="split",
    )(ensemble.reshape(rows * patches, values))
    arrived = [
        lax.all_to_all(piece, "member", split_axis=0, concat_axis=0, tiled=True)
        for piece in pieces
    ]

    smem = pl.BlockSpec(memory_space=pltpu.SMEM)
    anywhere = pl.BlockSpec(memory_space=pl.ANY)
    gram = pl.pallas_call(
        functools.partial(gram_kernel, 1.0 / (2.0 * size)),
        out_shape=jax.ShapeDtypeStruct((size, size), jnp.bfloat16),
        in_specs=[smem] * 3 + [anywhere] * 3,
        out_specs=vmem(),
        scratch_shapes=[
            pltpu.VMEM((slots * store.shape[1], size), jnp.bfloat16),
            pltpu.SemaphoreType.DMA((slots,)),
        ],
        compiler_params=params(),
        cost_estimate=cost(2 * slots * store.shape[1] * size * size, 4 * size * size),
        name="gram",
    )(
        block_ids.reshape(slots),
        block_src.reshape(slots),
        block_count.reshape(1),
        below,
        store,
        above,
    )

    returned = []
    for piece in arrived:
        moved = pl.pallas_call(
            transform_kernel,
            out_shape=jax.ShapeDtypeStruct((size, width), jnp.bfloat16),
            in_specs=[vmem()] * 2,
            out_specs=vmem(),
            scratch_shapes=[pltpu.VMEM((size, width), jnp.bfloat16)],
            compiler_params=params(),
            cost_estimate=cost(4 * size * size * width, 2 * size * size + 4 * size * width),
            name="transform",
        )(gram, piece.reshape(size, width))
        returned.append(
            lax.all_to_all(
                moved.reshape(patches, rows, width),
                "member",
                split_axis=0,
                concat_axis=0,
                tiled=True,
            )
        )

    fresh = pl.pallas_call(
        functools.partial(merge_kernel, patches),
        out_shape=jax.ShapeDtypeStruct((rows * patches, values), jnp.bfloat16),
        in_specs=[vmem()] * CHUNKS,
        out_specs=vmem(),
        compiler_params=params(),
        cost_estimate=cost(2 * 256 * rows * patches * values, 4 * rows * patches * values),
        name="merge",
    )(*returned)
    return fresh.reshape(ensemble.shape)


def solution(mesh):
    return jax.shard_map(
        shards,
        mesh=mesh,
        in_specs=(
            P("member", "region", None, None),
            P("region", "member", None, None, None),
            P("region", "member", None),
            P("region", "member", None),
            P("region", "member"),
        ),
        out_specs=P("member", "region", None, None),
        check_vma=False,
    )
```

```python
import functools

import jax
import jax.numpy as jnp
from jax import lax
from jax.experimental import pallas as pl
from jax.experimental.pallas import tpu as pltpu
from jax.sharding import PartitionSpec as P

LIMIT = 40 * 1024 * 1024


def rows_per_group(rows, patches):
    return min(rows, max(16, 256 // patches))


def partners(count):
    return list(range(count - 1, 0, -1))


def ppermute(value, axis, step):
    count = lax.axis_size(axis)
    return lax.ppermute(value, axis, [(i, i ^ step) for i in range(count)])


def split_kernel(me_ref, members_ref, *out_refs):
    patches = len(out_refs)
    rows = out_refs[0].shape[0]
    group = rows_per_group(rows, patches)
    height = group * patches
    row = lax.broadcasted_iota(jnp.int32, (height, height), 0)
    column = lax.broadcasted_iota(jnp.int32, (height, height), 1)
    source = lax.rem(row, group) * patches + (lax.div(row, group) ^ me_ref[0])
    shuffle = jnp.where(column == source, 1.0, 0.0).astype(jnp.bfloat16)
    for step in range(rows // group):
        block = members_ref[step * height : (step + 1) * height, :]
        moved = jnp.dot(shuffle, block, preferred_element_type=jnp.float32)
        moved = moved.astype(jnp.bfloat16)
        for k, out_ref in enumerate(out_refs):
            out_ref[step * group : (step + 1) * group, :] = moved[k * group : (k + 1) * group, :]


def merge_kernel(me_ref, *refs):
    piece_refs, out_ref = refs[:-1], refs[-1]
    patches = len(piece_refs)
    rows = piece_refs[0].shape[0]
    group = rows_per_group(rows, patches)
    height = group * patches
    row = lax.broadcasted_iota(jnp.int32, (height, height), 0)
    column = lax.broadcasted_iota(jnp.int32, (height, height), 1)
    source = (lax.rem(row, patches) ^ me_ref[0]) * group + lax.div(row, patches)
    shuffle = jnp.where(column == source, 1.0, 0.0).astype(jnp.bfloat16)
    for step in range(rows // group):
        here = slice(step * group, (step + 1) * group)
        block = jnp.concatenate([piece_ref[here, :] for piece_ref in piece_refs], axis=0)
        moved = jnp.dot(shuffle, block, preferred_element_type=jnp.float32)
        out_ref[step * height : (step + 1) * height, :] = moved.astype(jnp.bfloat16)


def gram_kernel(scale, ids_ref, src_ref, count_ref, below, own, above, gram_ref, stacked, sem):
    slots = ids_ref.shape[0]
    rows = own.shape[1]
    for slot in range(slots):
        live = slot < count_ref[0]
        target = stacked.at[pl.ds(slot * rows, rows), :]
        for code, store in enumerate((below, own, above)):

            @pl.when(live & (src_ref[slot] == code))
            def _():
                pltpu.make_async_copy(store.at[ids_ref[slot]], target, sem.at[slot]).start()

        @pl.when(jnp.logical_not(live))
        def _():
            target[...] = jnp.zeros(target.shape, target.dtype)

    for slot in range(slots):

        @pl.when(slot < count_ref[0])
        def _():
            target = stacked.at[pl.ds(slot * rows, rows), :]
            pltpu.make_async_copy(own.at[0], target, sem.at[slot]).wait()

    size = gram_ref.shape[0]
    part = min(size, 256)
    for step in range(size // part):
        block = lax.dot_general(
            stacked[:, step * part : (step + 1) * part],
            stacked[...],
            (((0,), (0,)), ((), ())),
            preferred_element_type=jnp.float32,
        )
        gram_ref[step * part : (step + 1) * part, :] = (block * scale).astype(jnp.bfloat16)


def transform_kernel(count, me_ref, gram_ref, *refs):
    piece_refs, out_refs = refs[:count], refs[count : 2 * count]
    members, first, fresh = refs[2 * count :]
    rows = piece_refs[0].shape[0]

    def place(k):
        return pl.ds(pl.multiple_of((me_ref[0] ^ k) * rows, rows), rows)

    for k in range(count):
        members[place(k), :] = piece_refs[k][...]
    size = gram_ref.shape[0]
    part = min(size, 256)
    for step in range(size // part):
        here = slice(step * part, (step + 1) * part)
        first[here, :] = jnp.dot(
            gram_ref[here, :], members[...], preferred_element_type=jnp.float32
        ).astype(jnp.bfloat16)
    for step in range(size // part):
        here = slice(step * part, (step + 1) * part)
        second = jnp.dot(gram_ref[here, :], first[...], preferred_element_type=jnp.float32)
        rest = members[here, :].astype(jnp.float32) - first[here, :].astype(jnp.float32)
        fresh[here, :] = (rest + second).astype(jnp.bfloat16)
    for k in range(count):
        out_refs[k][...] = fresh[place(k), :]


def vmem():
    return pl.BlockSpec(memory_space=pltpu.VMEM)


def params():
    return pltpu.CompilerParams(vmem_limit_bytes=LIMIT)


def cost(flops, nbytes):
    return pl.CostEstimate(flops=flops, bytes_accessed=nbytes, transcendentals=0)


def neighbours(store):
    count = lax.axis_size("region")
    up = [(i, i + 1) for i in range(count - 1)]
    down = [(i + 1, i) for i in range(count - 1)]
    return lax.ppermute(store, "region", up), lax.ppermute(store, "region", down)


def shards(ensemble, obs_store, block_ids, block_src, block_count):
    rows, _, patches, values = ensemble.shape
    store = obs_store.reshape(obs_store.shape[2:])
    size = store.shape[2]
    slots = block_ids.shape[2]
    me = lax.axis_index("member").astype(jnp.int32).reshape(1)
    below, above = neighbours(store)
    smem = pl.BlockSpec(memory_space=pltpu.SMEM)
    anywhere = pl.BlockSpec(memory_space=pl.ANY)
    piece_shape = jax.ShapeDtypeStruct((rows, values), jnp.bfloat16)

    pieces = pl.pallas_call(
        split_kernel,
        out_shape=[piece_shape] * patches,
        in_specs=[smem, vmem()],
        out_specs=[vmem()] * patches,
        compiler_params=params(),
        cost_estimate=cost(2 * 256 * rows * patches * values, 4 * rows * patches * values),
        name="split",
    )(me, ensemble.reshape(rows * patches, values))
    arrived = [pieces[0]] + [None] * (patches - 1)
    for k in partners(patches):
        arrived[k] = ppermute(pieces[k], "member", k)

    gram = pl.pallas_call(
        functools.partial(gram_kernel, 1.0 / (2.0 * size)),
        out_shape=jax.ShapeDtypeStruct((size, size), jnp.bfloat16),
        in_specs=[smem] * 3 + [anywhere] * 3,
        out_specs=vmem(),
        scratch_shapes=[
            pltpu.VMEM((slots * store.shape[1], size), jnp.bfloat16),
            pltpu.SemaphoreType.DMA((slots,)),
        ],
        compiler_params=params(),
        cost_estimate=cost(2 * slots * store.shape[1] * size * size, 4 * size * size),
        name="gram",
    )(
        block_ids.reshape(slots),
        block_src.reshape(slots),
        block_count.reshape(1),
        below,
        store,
        above,
    )

    moved = pl.pallas_call(
        functools.partial(transform_kernel, patches),
        out_shape=[piece_shape] * patches,
        in_specs=[smem] + [vmem()] * (1 + patches),
        out_specs=[vmem()] * patches,
        scratch_shapes=[pltpu.VMEM((size, values), jnp.bfloat16)] * 3,
        compiler_params=params(),
        cost_estimate=cost(4 * size * size * values, 2 * size * size + 4 * size * values),
        name="transform",
    )(me, gram, *arrived)
    returned = [moved[0]] + [None] * (patches - 1)
    for k in partners(patches):
        returned[k] = ppermute(moved[k], "member", k)

    fresh = pl.pallas_call(
        merge_kernel,
        out_shape=jax.ShapeDtypeStruct((rows * patches, values), jnp.bfloat16),
        in_specs=[smem] + [vmem()] * patches,
        out_specs=vmem(),
        compiler_params=params(),
        cost_estimate=cost(2 * 256 * rows * patches * values, 4 * rows * patches * values),
        name="merge",
    )(me, *returned)
    return fresh.reshape(ensemble.shape)


def solution(mesh):
    return jax.shard_map(
        shards,
        mesh=mesh,
        in_specs=(
            P("member", "region", None, None),
            P("region", "member", None, None, None),
            P("region", "member", None),
            P("region", "member", None),
            P("region", "member"),
        ),
        out_specs=P("member", "region", None, None),
        check_vma=False,
    )
```

```python
import functools

import jax
import jax.numpy as jnp
from jax import lax
from jax.experimental import pallas as pl
from jax.experimental.pallas import tpu as pltpu
from jax.sharding import PartitionSpec as P

LIMIT = 40 * 1024 * 1024


def rows_per_group(rows, patches):
    return min(rows, max(16, 256 // patches))


def partners(count):
    far = list(range(count - 1, count // 2 - 1, -1))
    near = list(range(count // 2 - 1, 0, -1))
    order = []
    for i in range(len(far)):
        order += far[i : i + 1] + near[i : i + 1]
    return order


def ppermute(value, axis, step):
    count = lax.axis_size(axis)
    return lax.ppermute(value, axis, [(i, i ^ step) for i in range(count)])


def split_kernel(me_ref, members_ref, *out_refs):
    patches = len(out_refs)
    rows = out_refs[0].shape[0]
    group = rows_per_group(rows, patches)
    height = group * patches
    row = lax.broadcasted_iota(jnp.int32, (height, height), 0)
    column = lax.broadcasted_iota(jnp.int32, (height, height), 1)
    source = lax.rem(row, group) * patches + (lax.div(row, group) ^ me_ref[0])
    shuffle = jnp.where(column == source, 1.0, 0.0).astype(jnp.bfloat16)
    for step in range(rows // group):
        block = members_ref[step * height : (step + 1) * height, :]
        moved = jnp.dot(shuffle, block, preferred_element_type=jnp.float32)
        moved = moved.astype(jnp.bfloat16)
        for k, out_ref in enumerate(out_refs):
            out_ref[step * group : (step + 1) * group, :] = moved[k * group : (k + 1) * group, :]


def merge_kernel(me_ref, *refs):
    piece_refs, out_ref = refs[:-1], refs[-1]
    patches = len(piece_refs)
    rows = piece_refs[0].shape[0]
    group = rows_per_group(rows, patches)
    height = group * patches
    row = lax.broadcasted_iota(jnp.int32, (height, height), 0)
    column = lax.broadcasted_iota(jnp.int32, (height, height), 1)
    source = (lax.rem(row, patches) ^ me_ref[0]) * group + lax.div(row, patches)
    shuffle = jnp.where(column == source, 1.0, 0.0).astype(jnp.bfloat16)
    for step in range(rows // group):
        here = slice(step * group, (step + 1) * group)
        block = jnp.concatenate([piece_ref[here, :] for piece_ref in piece_refs], axis=0)
        moved = jnp.dot(shuffle, block, preferred_element_type=jnp.float32)
        out_ref[step * height : (step + 1) * height, :] = moved.astype(jnp.bfloat16)


def gram_kernel(
    scale, region_ref, ids_hbm, src_hbm, count_hbm, own, even, odd, gram_ref,
    ids_ref, src_ref, count_ref, stacked, table_sem, sem,
):
    tables = [
        pltpu.make_async_copy(hbm, smem, table_sem.at[i])
        for i, (hbm, smem) in enumerate(
            ((ids_hbm, ids_ref), (src_hbm, src_ref), (count_hbm, count_ref))
        )
    ]
    for copy in tables:
        copy.start()
    for copy in tables:
        copy.wait()
    slots = ids_ref.shape[2]
    rows = own.shape[1]
    parity = lax.rem(region_ref[0], 2)
    count = count_ref[0, 0]
    for slot in range(slots):
        live = slot < count
        target = stacked.at[pl.ds(slot * rows, rows), :]
        source = src_ref[0, 0, slot]
        where = jnp.where(source == 1, 0, jnp.where((source == 2) == (parity == 0), 1, 2))
        for code, store in enumerate((own, even, odd)):

            @pl.when(live & (where == code))
            def _():
                block = store.at[ids_ref[0, 0, slot]]
                pltpu.make_async_copy(block, target, sem.at[slot]).start()

        @pl.when(jnp.logical_not(live))
        def _():
            target[...] = jnp.zeros(target.shape, target.dtype)

    for slot in range(slots):

        @pl.when(slot < count)
        def _():
            target = stacked.at[pl.ds(slot * rows, rows), :]
            pltpu.make_async_copy(own.at[0], target, sem.at[slot]).wait()

    size = gram_ref.shape[0]
    part = min(size, 256)
    for step in range(size // part):
        block = lax.dot_general(
            stacked[:, step * part : (step + 1) * part],
            stacked[...],
            (((0,), (0,)), ((), ())),
            preferred_element_type=jnp.float32,
        )
        gram_ref[step * part : (step + 1) * part, :] = (block * scale).astype(jnp.bfloat16)


def transform_kernel(count, me_ref, gram_ref, *refs):
    piece_refs, out_refs = refs[:count], refs[count : 2 * count]
    members, first, fresh = refs[2 * count :]
    rows = piece_refs[0].shape[0]

    def place(k):
        return pl.ds(pl.multiple_of((me_ref[0] ^ k) * rows, rows), rows)

    for k in range(count):
        members[place(k), :] = piece_refs[k][...]
    size = gram_ref.shape[0]
    part = min(size, 256)
    for step in range(size // part):
        here = slice(step * part, (step + 1) * part)
        first[here, :] = jnp.dot(
            gram_ref[here, :], members[...], preferred_element_type=jnp.float32
        ).astype(jnp.bfloat16)
    for step in range(size // part):
        here = slice(step * part, (step + 1) * part)
        second = jnp.dot(gram_ref[here, :], first[...], preferred_element_type=jnp.float32)
        rest = members[here, :].astype(jnp.float32) - first[here, :].astype(jnp.float32)
        fresh[here, :] = (rest + second).astype(jnp.bfloat16)
    for k in range(count):
        out_refs[k][...] = fresh[place(k), :]


def vmem():
    return pl.BlockSpec(memory_space=pltpu.VMEM)


def params():
    return pltpu.CompilerParams(vmem_limit_bytes=LIMIT)


def cost(flops, nbytes):
    return pl.CostEstimate(flops=flops, bytes_accessed=nbytes, transcendentals=0)


def neighbours(store):
    count = lax.axis_size("region")
    even = [(i, i ^ 1) for i in range(count) if i ^ 1 < count]
    odd = [(i, ((i + 1) ^ 1) - 1) for i in range(count) if 0 <= ((i + 1) ^ 1) - 1 < count]
    return lax.ppermute(store, "region", even), lax.ppermute(store, "region", odd)


def shards(ensemble, obs_store, block_ids, block_src, block_count):
    rows, _, patches, values = ensemble.shape
    store = obs_store.reshape(obs_store.shape[2:])
    size = store.shape[2]
    slots = block_ids.shape[2]
    me = lax.axis_index("member").astype(jnp.int32).reshape(1)
    region = lax.axis_index("region").astype(jnp.int32).reshape(1)
    smem = pl.BlockSpec(memory_space=pltpu.SMEM)
    hbm = pl.BlockSpec(memory_space=pltpu.HBM)
    piece_shape = jax.ShapeDtypeStruct((rows, values), jnp.bfloat16)

    pieces = pl.pallas_call(
        split_kernel,
        out_shape=[piece_shape] * patches,
        in_specs=[smem, vmem()],
        out_specs=[vmem()] * patches,
        compiler_params=params(),
        cost_estimate=cost(2 * 256 * rows * patches * values, 4 * rows * patches * values),
        name="split",
    )(me, ensemble.reshape(rows * patches, values))
    store, pieces = lax.optimization_barrier((store, pieces))
    even, odd = neighbours(store)
    arrived = [pieces[0]] + [None] * (patches - 1)
    for k in partners(patches):
        arrived[k] = ppermute(pieces[k], "member", k)

    gram = pl.pallas_call(
        functools.partial(gram_kernel, 1.0 / (2.0 * size)),
        out_shape=jax.ShapeDtypeStruct((size, size), jnp.bfloat16),
        in_specs=[smem] + [hbm] * 6,
        out_specs=vmem(),
        scratch_shapes=[
            pltpu.SMEM(block_ids.shape, jnp.int32),
            pltpu.SMEM(block_src.shape, jnp.int32),
            pltpu.SMEM(block_count.shape, jnp.int32),
            pltpu.VMEM((slots * store.shape[1], size), jnp.bfloat16),
            pltpu.SemaphoreType.DMA((3,)),
            pltpu.SemaphoreType.DMA((slots,)),
        ],
        compiler_params=params(),
        cost_estimate=cost(2 * slots * store.shape[1] * size * size, 4 * size * size),
        name="gram",
    )(region, block_ids, block_src, block_count, store, even, odd)

    moved = pl.pallas_call(
        functools.partial(transform_kernel, patches),
        out_shape=[piece_shape] * patches,
        in_specs=[smem] + [vmem()] * (1 + patches),
        out_specs=[vmem()] * patches,
        scratch_shapes=[pltpu.VMEM((size, values), jnp.bfloat16)] * 3,
        compiler_params=params(),
        cost_estimate=cost(4 * size * size * values, 2 * size * size + 4 * size * values),
        name="transform",
    )(me, gram, *arrived)
    returned = [moved[0]] + [None] * (patches - 1)
    for k in partners(patches):
        returned[k] = ppermute(moved[k], "member", k)

    fresh = pl.pallas_call(
        merge_kernel,
        out_shape=jax.ShapeDtypeStruct((rows * patches, values), jnp.bfloat16),
        in_specs=[smem] + [vmem()] * patches,
        out_specs=vmem(),
        compiler_params=params(),
        cost_estimate=cost(2 * 256 * rows * patches * values, 4 * rows * patches * values),
        name="merge",
    )(me, *returned)
    return fresh.reshape(ensemble.shape)


def solution(mesh):
    return jax.shard_map(
        shards,
        mesh=mesh,
        in_specs=(
            P("member", "region", None, None),
            P("region", "member", None, None, None),
            P("region", "member", None),
            P("region", "member", None),
            P("region", "member"),
        ),
        out_specs=P("member", "region", None, None),
        check_vma=False,
    )
```

```python
import functools

import jax
import jax.numpy as jnp
from jax import lax
from jax.experimental import pallas as pl
from jax.experimental.pallas import tpu as pltpu
from jax.sharding import PartitionSpec as P

EARLY = 2
LIMIT = 16 * 1024 * 1024


def rows_per_group(rows, patches):
    return min(rows, max(16, 256 // patches))


def partners(count):
    far = list(range(count - 1, count // 2 - 1, -1))
    near = list(range(count // 2 - 1, 0, -1))
    order = []
    for i in range(len(far)):
        order += far[i : i + 1] + near[i : i + 1]
    return order + [0]


def ppermute(value, axis, step):
    if step == 0:
        return value
    count = lax.axis_size(axis)
    return lax.ppermute(value, axis, [(i, i ^ step) for i in range(count)])


def split_kernel(me_ref, members_ref, *out_refs):
    patches = len(out_refs)
    rows = out_refs[0].shape[0]
    group = rows_per_group(rows, patches)
    height = group * patches
    row = lax.broadcasted_iota(jnp.int32, (height, height), 0)
    column = lax.broadcasted_iota(jnp.int32, (height, height), 1)
    source = lax.rem(row, group) * patches + (lax.div(row, group) ^ me_ref[0])
    shuffle = jnp.where(column == source, 1.0, 0.0).astype(jnp.bfloat16)
    for step in range(rows // group):
        block = members_ref[step * height : (step + 1) * height, :]
        moved = jnp.dot(shuffle, block, preferred_element_type=jnp.float32)
        moved = moved.astype(jnp.bfloat16)
        for k, out_ref in enumerate(out_refs):
            out_ref[step * group : (step + 1) * group, :] = moved[k * group : (k + 1) * group, :]


def merge_kernel(order, me_ref, *refs):
    patches = len(order)
    piece_refs, out_ref = dict(zip(order, refs)), refs[-1]
    rows = piece_refs[0].shape[0]
    group = rows_per_group(rows, patches)
    height = group * patches
    row = lax.broadcasted_iota(jnp.int32, (height, height), 0)
    column = lax.broadcasted_iota(jnp.int32, (height, height), 1)
    source = (lax.rem(row, patches) ^ me_ref[0]) * group + lax.div(row, patches)
    shuffle = jnp.where(column == source, 1.0, 0.0).astype(jnp.bfloat16)
    for step in range(rows // group):
        here = slice(step * group, (step + 1) * group)
        block = jnp.concatenate([piece_refs[k][here, :] for k in range(patches)], axis=0)
        moved = jnp.dot(shuffle, block, preferred_element_type=jnp.float32)
        out_ref[step * height : (step + 1) * height, :] = moved.astype(jnp.bfloat16)


def gram_kernel(
    scale, region_ref, ids_hbm, src_hbm, count_hbm, own, even, odd, gram_ref,
    ids_ref, src_ref, count_ref, stacked, table_sem, sem,
):
    tables = [
        pltpu.make_async_copy(hbm, smem, table_sem.at[i])
        for i, (hbm, smem) in enumerate(
            ((ids_hbm, ids_ref), (src_hbm, src_ref), (count_hbm, count_ref))
        )
    ]
    for copy in tables:
        copy.start()
    for copy in tables:
        copy.wait()
    slots = ids_ref.shape[2]
    rows = own.shape[1]
    parity = lax.rem(region_ref[0], 2)
    count = count_ref[0, 0]
    for slot in range(slots):
        live = slot < count
        target = stacked.at[pl.ds(slot * rows, rows), :]
        source = src_ref[0, 0, slot]
        where = jnp.where(source == 1, 0, jnp.where((source == 2) == (parity == 0), 1, 2))
        for code, store in enumerate((own, even, odd)):

            @pl.when(live & (where == code))
            def _():
                block = store.at[ids_ref[0, 0, slot]]
                pltpu.make_async_copy(block, target, sem.at[slot]).start()

        @pl.when(jnp.logical_not(live))
        def _():
            target[...] = jnp.zeros(target.shape, target.dtype)

    for slot in range(slots):

        @pl.when(slot < count)
        def _():
            target = stacked.at[pl.ds(slot * rows, rows), :]
            pltpu.make_async_copy(own.at[0], target, sem.at[slot]).wait()

    size = gram_ref.shape[0]
    part = min(size, 256)
    for step in range(size // part):
        block = lax.dot_general(
            stacked[:, step * part : (step + 1) * part],
            stacked[...],
            (((0,), (0,)), ((), ())),
            preferred_element_type=jnp.float32,
        )
        gram_ref[step * part : (step + 1) * part, :] = (block * scale).astype(jnp.bfloat16)


def transform_kernel(order, me_ref, *refs):
    count = len(order)
    piece_refs = dict(zip(order, refs[:EARLY] + refs[EARLY + 1 : count + 1]))
    gram_ref, out_refs = refs[EARLY], refs[count + 1 : 2 * count + 1]
    members, first, fresh = refs[2 * count + 1 :]
    rows = out_refs[0].shape[0]

    def place(k):
        return pl.ds(pl.multiple_of((me_ref[0] ^ k) * rows, rows), rows)

    for k in range(count):
        members[place(k), :] = piece_refs[k][...]
    size = gram_ref.shape[0]
    part = min(size, 256)
    for step in range(size // part):
        here = slice(step * part, (step + 1) * part)
        first[here, :] = jnp.dot(
            gram_ref[here, :], members[...], preferred_element_type=jnp.float32
        ).astype(jnp.bfloat16)
    for step in range(size // part):
        here = slice(step * part, (step + 1) * part)
        second = jnp.dot(gram_ref[here, :], first[...], preferred_element_type=jnp.float32)
        rest = members[here, :].astype(jnp.float32) - first[here, :].astype(jnp.float32)
        fresh[here, :] = (rest + second).astype(jnp.bfloat16)
    for k in range(count):
        out_refs[k][...] = fresh[place(k), :]


def vmem():
    return pl.BlockSpec(memory_space=pltpu.VMEM)


def params():
    return pltpu.CompilerParams(vmem_limit_bytes=LIMIT)


def cost(flops, nbytes):
    return pl.CostEstimate(flops=flops, bytes_accessed=nbytes, transcendentals=0)


def neighbours(store):
    count = lax.axis_size("region")
    even = [(i, i ^ 1) for i in range(count) if i ^ 1 < count]
    odd = [(i, ((i + 1) ^ 1) - 1) for i in range(count) if 0 <= ((i + 1) ^ 1) - 1 < count]
    return lax.ppermute(store, "region", even), lax.ppermute(store, "region", odd)


def shards(ensemble, obs_store, block_ids, block_src, block_count):
    rows, _, patches, values = ensemble.shape
    store = obs_store.reshape(obs_store.shape[2:])
    size = store.shape[2]
    slots = block_ids.shape[2]
    me = lax.axis_index("member").astype(jnp.int32).reshape(1)
    region = lax.axis_index("region").astype(jnp.int32).reshape(1)
    smem = pl.BlockSpec(memory_space=pltpu.SMEM)
    hbm = pl.BlockSpec(memory_space=pltpu.HBM)
    piece_shape = jax.ShapeDtypeStruct((rows, values), jnp.bfloat16)

    pieces = pl.pallas_call(
        split_kernel,
        out_shape=[piece_shape] * patches,
        in_specs=[smem, vmem()],
        out_specs=[vmem()] * patches,
        compiler_params=params(),
        cost_estimate=cost(2 * 256 * rows * patches * values, 4 * rows * patches * values),
        name="split",
    )(me, ensemble.reshape(rows * patches, values))
    store, pieces = lax.optimization_barrier((store, pieces))
    even, odd = neighbours(store)
    order = partners(patches)
    arrived = [ppermute(pieces[k], "member", k) for k in order]

    gram = pl.pallas_call(
        functools.partial(gram_kernel, 1.0 / (2.0 * size)),
        out_shape=jax.ShapeDtypeStruct((size, size), jnp.bfloat16),
        in_specs=[smem] + [hbm] * 6,
        out_specs=vmem(),
        scratch_shapes=[
            pltpu.SMEM(block_ids.shape, jnp.int32),
            pltpu.SMEM(block_src.shape, jnp.int32),
            pltpu.SMEM(block_count.shape, jnp.int32),
            pltpu.VMEM((slots * store.shape[1], size), jnp.bfloat16),
            pltpu.SemaphoreType.DMA((3,)),
            pltpu.SemaphoreType.DMA((slots,)),
        ],
        compiler_params=params(),
        cost_estimate=cost(2 * slots * store.shape[1] * size * size, 4 * size * size),
        name="gram",
    )(region, block_ids, block_src, block_count, store, even, odd)

    moved = pl.pallas_call(
        functools.partial(transform_kernel, order),
        out_shape=[piece_shape] * patches,
        in_specs=[smem] + [vmem()] * (1 + patches),
        out_specs=[vmem()] * patches,
        scratch_shapes=[pltpu.VMEM((size, values), jnp.bfloat16)] * 3,
        compiler_params=params(),
        cost_estimate=cost(4 * size * size * values, 2 * size * size + 4 * size * values),
        name="transform",
    )(me, *arrived[:EARLY], gram, *arrived[EARLY:])
    returned = [ppermute(moved[k], "member", k) for k in order]

    fresh = pl.pallas_call(
        functools.partial(merge_kernel, order),
        out_shape=jax.ShapeDtypeStruct((rows * patches, values), jnp.bfloat16),
        in_specs=[smem] + [vmem()] * patches,
        out_specs=vmem(),
        compiler_params=params(),
        cost_estimate=cost(2 * 256 * rows * patches * values, 4 * rows * patches * values),
        name="merge",
    )(me, *returned)
    return fresh.reshape(ensemble.shape)


def solution(mesh):
    return jax.shard_map(
        shards,
        mesh=mesh,
        in_specs=(
            P("member", "region", None, None),
            P("region", "member", None, None, None),
            P("region", "member", None),
            P("region", "member", None),
            P("region", "member"),
        ),
        out_specs=P("member", "region", None, None),
        check_vma=False,
    )
```

```python
import functools

import jax
import jax.numpy as jnp
from jax import lax
from jax.experimental import pallas as pl
from jax.experimental.pallas import tpu as pltpu
from jax.sharding import PartitionSpec as P

SHARES = (1, 1)
CHUNKS = len(SHARES)
EARLY = 7
LIMIT = 16 * 1024 * 1024


def rows_per_group(rows, patches):
    return min(rows, max(16, 256 // patches))


def far_steps(count):
    return list(range(count - 1, count // 2 - 1, -1))


def near_steps(count):
    return list(range(count // 2 - 1, 0, -1)) + [0]


def span(values, chunk):
    unit = values // sum(SHARES)
    start = sum(SHARES[:chunk]) * unit
    return slice(start, start + SHARES[chunk] * unit)


def ppermute(value, axis, step):
    if step == 0:
        return value
    count = lax.axis_size(axis)
    return lax.ppermute(value, axis, [(i, i ^ step) for i in range(count)])


def after(value, *earlier):
    return lax.optimization_barrier((value, *earlier))[0] if earlier else value


def inward_waits(count):
    far, near = far_steps(count), near_steps(count)[:-1]
    waits = {far[i]: [far[i - 2]] for i in range(2, len(far))}
    for i, k in enumerate(near[:-1]):
        waits[k] = [far[i]]
    return waits


def outward_waits(count):
    far, near = far_steps(count), near_steps(count)[:-1]
    line = [(k, chunk) for chunk in range(CHUNKS) for k in far]
    waits = {line[i]: [line[i - 2]] for i in range(2, len(line))}
    for chunk in range(CHUNKS):
        for i, k in enumerate(near):
            waits[(k, chunk)] = [(far[i], chunk)]
            if chunk + 1 < CHUNKS:
                waits[(far[i], chunk + 1)].append((k, chunk))
    return waits


def split_kernel(keys, patches, me_ref, members_ref, *out_refs):
    rows = out_refs[0].shape[0]
    group = rows_per_group(rows, patches)
    height = group * patches
    base = min(keys)
    tall = (1 + max(keys) - base) * group
    row = lax.broadcasted_iota(jnp.int32, (tall, height), 0)
    column = lax.broadcasted_iota(jnp.int32, (tall, height), 1)
    source = lax.rem(row, group) * patches + ((base + lax.div(row, group)) ^ me_ref[0])
    shuffle = jnp.where(column == source, 1.0, 0.0).astype(jnp.bfloat16)
    for step in range(rows // group):
        block = members_ref[step * height : (step + 1) * height, :]
        moved = jnp.dot(shuffle, block, preferred_element_type=jnp.float32)
        moved = moved.astype(jnp.bfloat16)
        here = slice(step * group, (step + 1) * group)
        for k, out_ref in zip(keys, out_refs):
            out_ref[here, :] = moved[(k - base) * group : (k - base + 1) * group, :]


def merge_kernel(keys, me_ref, *refs):
    pieces, out_ref = dict(zip(keys, refs)), refs[-1]
    patches = 1 + max(k for k, _ in keys)
    rows = out_ref.shape[0] // patches
    values = out_ref.shape[1]
    group = rows_per_group(rows, patches)
    height = group * patches
    row = lax.broadcasted_iota(jnp.int32, (height, height), 0)
    column = lax.broadcasted_iota(jnp.int32, (height, height), 1)
    source = (lax.rem(row, patches) ^ me_ref[0]) * group + lax.div(row, patches)
    shuffle = jnp.where(column == source, 1.0, 0.0).astype(jnp.bfloat16)
    for step in range(rows // group):
        here = slice(step * group, (step + 1) * group)
        for chunk in range(CHUNKS):
            parts = [pieces[(k, chunk)][here, :] for k in range(patches)]
            block = jnp.concatenate(parts, axis=0)
            moved = jnp.dot(shuffle, block, preferred_element_type=jnp.float32)
            out_ref[step * height : (step + 1) * height, span(values, chunk)] = moved.astype(
                jnp.bfloat16
            )


def gram_kernel(
    scale, region_ref, ids_hbm, src_hbm, count_hbm, own, even, odd, gram_ref,
    ids_ref, src_ref, count_ref, stacked, table_sem, sem,
):
    tables = [
        pltpu.make_async_copy(hbm, smem, table_sem.at[i])
        for i, (hbm, smem) in enumerate(
            ((ids_hbm, ids_ref), (src_hbm, src_ref), (count_hbm, count_ref))
        )
    ]
    for copy in tables:
        copy.start()
    for copy in tables:
        copy.wait()
    slots = ids_ref.shape[2]
    rows = own.shape[1]
    parity = lax.rem(region_ref[0], 2)
    count = count_ref[0, 0]
    for slot in range(slots):
        live = slot < count
        target = stacked.at[pl.ds(slot * rows, rows), :]
        source = src_ref[0, 0, slot]
        where = jnp.where(source == 1, 0, jnp.where((source == 2) == (parity == 0), 1, 2))
        for code, store in enumerate((own, even, odd)):

            @pl.when(live & (where == code))
            def _():
                block = store.at[ids_ref[0, 0, slot]]
                pltpu.make_async_copy(block, target, sem.at[slot]).start()

        @pl.when(jnp.logical_not(live))
        def _():
            target[...] = jnp.zeros(target.shape, target.dtype)

    for slot in range(slots):

        @pl.when(slot < count)
        def _():
            target = stacked.at[pl.ds(slot * rows, rows), :]
            pltpu.make_async_copy(own.at[0], target, sem.at[slot]).wait()

    total = lax.dot_general(
        stacked[...], stacked[...], (((0,), (0,)), ((), ())), preferred_element_type=jnp.float32
    )
    gram_ref[...] = (total * scale).astype(jnp.bfloat16)


def transform_kernel(values, chunk, keys, out_keys, me_ref, *refs):
    count = len(keys)
    pieces = dict(zip(keys, refs[:EARLY] + refs[EARLY + 1 : count + 1]))
    gram_ref, out_refs = refs[EARLY], refs[count + 1 : -3]
    members, first, fresh = refs[-3:]
    rows = gram_ref.shape[0] // count

    def place(k):
        return pl.ds(pl.multiple_of((me_ref[0] ^ k) * rows, rows), rows)

    for k, piece in pieces.items():
        members[place(k), :] = piece[:, span(values, chunk)]
    gram = gram_ref[...]
    first[...] = jnp.dot(gram, members[...], preferred_element_type=jnp.float32).astype(
        jnp.bfloat16
    )
    second = jnp.dot(gram, first[...], preferred_element_type=jnp.float32)
    rest = members[...].astype(jnp.float32) - first[...].astype(jnp.float32)
    fresh[...] = (rest + second).astype(jnp.bfloat16)
    for k, out_ref in zip(out_keys, out_refs):
        out_ref[...] = fresh[place(k), :]


def vmem():
    return pl.BlockSpec(memory_space=pltpu.VMEM)


def params():
    return pltpu.CompilerParams(vmem_limit_bytes=LIMIT)


def cost(flops, nbytes):
    return pl.CostEstimate(flops=flops, bytes_accessed=nbytes, transcendentals=0)


def neighbours(store):
    count = lax.axis_size("region")
    even = [(i, i ^ 1) for i in range(count) if i ^ 1 < count]
    odd = [(i, ((i + 1) ^ 1) - 1) for i in range(count) if 0 <= ((i + 1) ^ 1) - 1 < count]
    return lax.ppermute(store, "region", even), lax.ppermute(store, "region", odd)


def shards(ensemble, obs_store, block_ids, block_src, block_count):
    rows, _, patches, values = ensemble.shape
    store = obs_store.reshape(obs_store.shape[2:])
    size = store.shape[2]
    slots = block_ids.shape[2]
    me = lax.axis_index("member").astype(jnp.int32).reshape(1)
    region = lax.axis_index("region").astype(jnp.int32).reshape(1)
    smem = pl.BlockSpec(memory_space=pltpu.SMEM)
    hbm = pl.BlockSpec(memory_space=pltpu.HBM)
    widths = [values * share // sum(SHARES) for share in SHARES]

    def piece_shape(width):
        return jax.ShapeDtypeStruct((rows, width), jnp.bfloat16)

    def split(keys, members):
        share = rows * patches * values
        return pl.pallas_call(
            functools.partial(split_kernel, keys, patches),
            out_shape=[piece_shape(values)] * len(keys),
            in_specs=[smem, vmem()],
            out_specs=[vmem()] * len(keys),
            compiler_params=params(),
            cost_estimate=cost(256 * share, 3 * share),
            name="split",
        )(me, members)

    far, near = far_steps(patches), near_steps(patches)
    steps = far + near
    members = ensemble.reshape(rows * patches, values)
    far_pieces = split(far, members)
    near_pieces = split(near, after(members, far_pieces[0]))
    arrived = {}
    waits = inward_waits(patches)
    for k, piece in zip(steps, far_pieces + near_pieces):
        earlier = [arrived[other] for other in waits.get(k, [])]
        arrived[k] = ppermute(after(piece, *earlier), "member", k)
    even, odd = neighbours(after(store, far_pieces[0]))

    gram = pl.pallas_call(
        functools.partial(gram_kernel, 1.0 / (2.0 * size)),
        out_shape=jax.ShapeDtypeStruct((size, size), jnp.bfloat16),
        in_specs=[smem] + [hbm] * 6,
        out_specs=vmem(),
        scratch_shapes=[
            pltpu.SMEM(block_ids.shape, jnp.int32),
            pltpu.SMEM(block_src.shape, jnp.int32),
            pltpu.SMEM(block_count.shape, jnp.int32),
            pltpu.VMEM((slots * store.shape[1], size), jnp.bfloat16),
            pltpu.SemaphoreType.DMA((3,)),
            pltpu.SemaphoreType.DMA((slots,)),
        ],
        compiler_params=params(),
        cost_estimate=cost(2 * slots * store.shape[1] * size * size, 4 * size * size),
        name="gram",
    )(region, block_ids, block_src, block_count, store, even, odd)

    returned = {}
    waits = outward_waits(patches)
    inputs = [arrived[k] for k in steps]
    for chunk in range(CHUNKS):
        width = widths[chunk]
        moved = pl.pallas_call(
            functools.partial(transform_kernel, values, chunk, steps, steps),
            out_shape=[piece_shape(width)] * len(steps),
            in_specs=[smem] + [vmem()] * (1 + len(steps)),
            out_specs=[vmem()] * len(steps),
            scratch_shapes=[pltpu.VMEM((size, width), jnp.bfloat16)] * 3,
            compiler_params=params(),
            cost_estimate=cost(4 * size * size * width, 2 * size * size + 4 * size * width),
            name="transform",
        )(me, *inputs[:EARLY], gram, *inputs[EARLY:])
        for k, piece in zip(steps, moved):
            earlier = [returned[other] for other in waits.get((k, chunk), [])]
            returned[(k, chunk)] = ppermute(after(piece, *earlier), "member", k)

    keys = [(k, chunk) for chunk in range(CHUNKS) for k in steps]
    fresh = pl.pallas_call(
        functools.partial(merge_kernel, keys),
        out_shape=jax.ShapeDtypeStruct((rows * patches, values), jnp.bfloat16),
        in_specs=[smem] + [vmem()] * len(keys),
        out_specs=vmem(),
        compiler_params=params(),
        cost_estimate=cost(2 * 256 * rows * patches * values, 4 * rows * patches * values),
        name="merge",
    )(me, *[returned[key] for key in keys])
    return fresh.reshape(ensemble.shape)


def solution(mesh):
    return jax.shard_map(
        shards,
        mesh=mesh,
        in_specs=(
            P("member", "region", None, None),
            P("region", "member", None, None, None),
            P("region", "member", None),
            P("region", "member", None),
            P("region", "member"),
        ),
        out_specs=P("member", "region", None, None),
        check_vma=False,
    )
```

```python
import functools

import jax
import jax.numpy as jnp
from jax import lax
from jax.experimental import pallas as pl
from jax.experimental.pallas import tpu as pltpu
from jax.sharding import PartitionSpec as P

EARLY = 2
LIMIT = 16 * 1024 * 1024


def rows_per_group(rows, patches):
    return min(rows, max(16, 256 // patches))


def partners(count):
    far = list(range(count - 1, count // 2 - 1, -1))
    near = list(range(count // 2 - 1, 0, -1))
    order = []
    for i in range(len(far)):
        order += far[i : i + 1] + near[i : i + 1]
    return order + [0]


def ppermute(value, axis, step):
    if step == 0:
        return value
    count = lax.axis_size(axis)
    return lax.ppermute(value, axis, [(i, i ^ step) for i in range(count)])


def split_kernel(me_ref, members_ref, *out_refs):
    patches = len(out_refs)
    rows = out_refs[0].shape[0]
    group = rows_per_group(rows, patches)
    height = group * patches
    row = lax.broadcasted_iota(jnp.int32, (height, height), 0)
    column = lax.broadcasted_iota(jnp.int32, (height, height), 1)
    source = lax.rem(row, group) * patches + (lax.div(row, group) ^ me_ref[0])
    shuffle = jnp.where(column == source, 1.0, 0.0).astype(jnp.bfloat16)
    for step in range(rows // group):
        block = members_ref[step * height : (step + 1) * height, :]
        moved = jnp.dot(shuffle, block, preferred_element_type=jnp.float32)
        moved = moved.astype(jnp.bfloat16)
        for k, out_ref in enumerate(out_refs):
            out_ref[step * group : (step + 1) * group, :] = moved[k * group : (k + 1) * group, :]


def merge_kernel(order, me_ref, *refs):
    patches = len(order)
    piece_refs, out_ref = dict(zip(order, refs)), refs[-1]
    rows = piece_refs[0].shape[0]
    group = rows_per_group(rows, patches)
    height = group * patches
    row = lax.broadcasted_iota(jnp.int32, (height, height), 0)
    column = lax.broadcasted_iota(jnp.int32, (height, height), 1)
    source = (lax.rem(row, patches) ^ me_ref[0]) * group + lax.div(row, patches)
    shuffle = jnp.where(column == source, 1.0, 0.0).astype(jnp.bfloat16)
    for step in range(rows // group):
        here = slice(step * group, (step + 1) * group)
        block = jnp.concatenate([piece_refs[k][here, :] for k in range(patches)], axis=0)
        moved = jnp.dot(shuffle, block, preferred_element_type=jnp.float32)
        out_ref[step * height : (step + 1) * height, :] = moved.astype(jnp.bfloat16)


def gram_kernel(
    scale, region_ref, ids_hbm, src_hbm, count_hbm, own, even, odd, gram_ref,
    ids_ref, src_ref, count_ref, stacked, table_sem, sem,
):
    tables = [
        pltpu.make_async_copy(hbm, smem, table_sem.at[i])
        for i, (hbm, smem) in enumerate(
            ((ids_hbm, ids_ref), (src_hbm, src_ref), (count_hbm, count_ref))
        )
    ]
    for copy in tables:
        copy.start()
    for copy in tables:
        copy.wait()
    slots = ids_ref.shape[2]
    rows = own.shape[1]
    parity = lax.rem(region_ref[0], 2)
    count = count_ref[0, 0]
    for slot in range(slots):
        live = slot < count
        target = stacked.at[pl.ds(slot * rows, rows), :]
        source = src_ref[0, 0, slot]
        where = jnp.where(source == 1, 0, jnp.where((source == 2) == (parity == 0), 1, 2))
        for code, store in enumerate((own, even, odd)):

            @pl.when(live & (where == code))
            def _():
                block = store.at[ids_ref[0, 0, slot]]
                pltpu.make_async_copy(block, target, sem.at[slot]).start()

        @pl.when(jnp.logical_not(live))
        def _():
            target[...] = jnp.zeros(target.shape, target.dtype)

    for slot in range(slots):

        @pl.when(slot < count)
        def _():
            target = stacked.at[pl.ds(slot * rows, rows), :]
            pltpu.make_async_copy(own.at[0], target, sem.at[slot]).wait()

    size = gram_ref.shape[0]
    part = min(size, 256)
    for step in range(size // part):
        block = lax.dot_general(
            stacked[:, step * part : (step + 1) * part],
            stacked[...],
            (((0,), (0,)), ((), ())),
            preferred_element_type=jnp.float32,
        )
        gram_ref[step * part : (step + 1) * part, :] = (block * scale).astype(jnp.bfloat16)


def transform_kernel(order, me_ref, *refs):
    count = len(order)
    piece_refs = dict(zip(order, refs[:EARLY] + refs[EARLY + 1 : count + 1]))
    gram_ref, out_refs = refs[EARLY], refs[count + 1 : 2 * count + 1]
    members, first, fresh = refs[2 * count + 1 :]
    rows = out_refs[0].shape[0]

    def place(k):
        return pl.ds(pl.multiple_of((me_ref[0] ^ k) * rows, rows), rows)

    for k in range(count):
        members[place(k), :] = piece_refs[k][...]
    size = gram_ref.shape[0]
    part = min(size, 256)
    for step in range(size // part):
        here = slice(step * part, (step + 1) * part)
        first[here, :] = jnp.dot(
            gram_ref[here, :], members[...], preferred_element_type=jnp.float32
        ).astype(jnp.bfloat16)
    for step in range(size // part):
        here = slice(step * part, (step + 1) * part)
        second = jnp.dot(gram_ref[here, :], first[...], preferred_element_type=jnp.float32)
        rest = members[here, :].astype(jnp.float32) - first[here, :].astype(jnp.float32)
        fresh[here, :] = (rest + second).astype(jnp.bfloat16)
    for k in range(count):
        out_refs[k][...] = fresh[place(k), :]


def vmem():
    return pl.BlockSpec(memory_space=pltpu.VMEM)


def params():
    return pltpu.CompilerParams(vmem_limit_bytes=LIMIT)


def cost(flops, nbytes):
    return pl.CostEstimate(flops=flops, bytes_accessed=nbytes, transcendentals=0)


def swap(store, first):
    count = lax.axis_size("region")
    pairs = [(i, i + 1) for i in range(first, count - 1, 2)]
    return lax.ppermute(store, "region", pairs + [(j, i) for i, j in pairs])


def shards(ensemble, obs_store, block_ids, block_src, block_count):
    rows, _, patches, values = ensemble.shape
    store = obs_store.reshape(obs_store.shape[2:])
    size = store.shape[2]
    slots = block_ids.shape[2]
    me = lax.axis_index("member").astype(jnp.int32).reshape(1)
    region = lax.axis_index("region").astype(jnp.int32).reshape(1)
    smem = pl.BlockSpec(memory_space=pltpu.SMEM)
    hbm = pl.BlockSpec(memory_space=pltpu.HBM)
    piece_shape = jax.ShapeDtypeStruct((rows, values), jnp.bfloat16)

    odd, even = swap(store, 1), swap(store, 0)
    pieces = pl.pallas_call(
        split_kernel,
        out_shape=[piece_shape] * patches,
        in_specs=[smem, vmem()],
        out_specs=[vmem()] * patches,
        compiler_params=params(),
        cost_estimate=cost(2 * 256 * rows * patches * values, 4 * rows * patches * values),
        name="split",
    )(me, ensemble.reshape(rows * patches, values))
    order = partners(patches)
    arrived = [ppermute(pieces[k], "member", k) for k in order]

    gram = pl.pallas_call(
        functools.partial(gram_kernel, 1.0 / (2.0 * size)),
        out_shape=jax.ShapeDtypeStruct((size, size), jnp.bfloat16),
        in_specs=[smem] + [hbm] * 6,
        out_specs=vmem(),
        scratch_shapes=[
            pltpu.SMEM(block_ids.shape, jnp.int32),
            pltpu.SMEM(block_src.shape, jnp.int32),
            pltpu.SMEM(block_count.shape, jnp.int32),
            pltpu.VMEM((slots * store.shape[1], size), jnp.bfloat16),
            pltpu.SemaphoreType.DMA((3,)),
            pltpu.SemaphoreType.DMA((slots,)),
        ],
        compiler_params=params(),
        cost_estimate=cost(2 * slots * store.shape[1] * size * size, 4 * size * size),
        name="gram",
    )(region, block_ids, block_src, block_count, store, even, odd)

    moved = pl.pallas_call(
        functools.partial(transform_kernel, order),
        out_shape=[piece_shape] * patches,
        in_specs=[smem] + [vmem()] * (1 + patches),
        out_specs=[vmem()] * patches,
        scratch_shapes=[pltpu.VMEM((size, values), jnp.bfloat16)] * 3,
        compiler_params=params(),
        cost_estimate=cost(4 * size * size * values, 2 * size * size + 4 * size * values),
        name="transform",
    )(me, *arrived[:EARLY], gram, *arrived[EARLY:])
    returned = [ppermute(moved[k], "member", k) for k in order]

    fresh = pl.pallas_call(
        functools.partial(merge_kernel, order),
        out_shape=jax.ShapeDtypeStruct((rows * patches, values), jnp.bfloat16),
        in_specs=[smem] + [vmem()] * patches,
        out_specs=vmem(),
        compiler_params=params(),
        cost_estimate=cost(2 * 256 * rows * patches * values, 4 * rows * patches * values),
        name="merge",
    )(me, *returned)
    return fresh.reshape(ensemble.shape)


def solution(mesh):
    return jax.shard_map(
        shards,
        mesh=mesh,
        in_specs=(
            P("member", "region", None, None),
            P("region", "member", None, None, None),
            P("region", "member", None),
            P("region", "member", None),
            P("region", "member"),
        ),
        out_specs=P("member", "region", None, None),
        check_vma=False,
    )
```

```python
import functools

import jax
import jax.numpy as jnp
from jax import lax
from jax.experimental import pallas as pl
from jax.experimental.pallas import tpu as pltpu
from jax.sharding import PartitionSpec as P

LIMIT = 16 * 1024 * 1024


def rows_per_group(rows, patches):
    return min(rows, max(16, 256 // patches))


PARTS = 8


def is_late(k, count):
    return k // (count // PARTS) == PARTS // 2


def partners(count):
    far = list(range(count - 1, count // 2 - 1, -1))
    near = list(range(count // 2 - 1, 0, -1))
    order = []
    for i in range(len(far)):
        order += far[i : i + 1] + near[i : i + 1]
    return order


def inward(count):
    order = [k for k in partners(count) if not is_late(k, count)]
    last_far = order.index(min(k for k in order if k >= count // 2))
    order.insert(min(3, last_far), order.pop(last_far))
    return order + [k for k in partners(count) if is_late(k, count)]


def ppermute(value, axis, step):
    if step == 0:
        return value
    count = lax.axis_size(axis)
    return lax.ppermute(value, axis, [(i, i ^ step) for i in range(count)])


def split_kernel(steps, me_ref, members_ref, *out_refs):
    patches = len(steps)
    rows = out_refs[0].shape[0]
    group = rows_per_group(rows, patches)
    height = group * patches
    row = lax.broadcasted_iota(jnp.int32, (height, height), 0)
    column = lax.broadcasted_iota(jnp.int32, (height, height), 1)
    source = lax.rem(row, group) * patches + (lax.div(row, group) ^ me_ref[0])
    shuffle = jnp.where(column == source, 1.0, 0.0).astype(jnp.bfloat16)
    for step in range(rows // group):
        block = members_ref[step * height : (step + 1) * height, :]
        moved = jnp.dot(shuffle, block, preferred_element_type=jnp.float32)
        moved = moved.astype(jnp.bfloat16)
        for k, out_ref in zip(steps, out_refs):
            out_ref[step * group : (step + 1) * group, :] = moved[k * group : (k + 1) * group, :]


def merge_kernel(order, me_ref, *refs):
    patches = len(order)
    piece_refs, out_ref = dict(zip(order, refs)), refs[-1]
    rows = piece_refs[0].shape[0]
    group = rows_per_group(rows, patches)
    height = group * patches
    row = lax.broadcasted_iota(jnp.int32, (height, height), 0)
    column = lax.broadcasted_iota(jnp.int32, (height, height), 1)
    source = (lax.rem(row, patches) ^ me_ref[0]) * group + lax.div(row, patches)
    shuffle = jnp.where(column == source, 1.0, 0.0).astype(jnp.bfloat16)
    for step in range(rows // group):
        here = slice(step * group, (step + 1) * group)
        block = jnp.concatenate([piece_refs[k][here, :] for k in range(patches)], axis=0)
        moved = jnp.dot(shuffle, block, preferred_element_type=jnp.float32)
        out_ref[step * height : (step + 1) * height, :] = moved.astype(jnp.bfloat16)


def gram_kernel(
    scale, region_ref, ids_hbm, src_hbm, count_hbm, own, even, odd, gram_ref,
    ids_ref, src_ref, count_ref, stacked, table_sem, sem,
):
    tables = [
        pltpu.make_async_copy(hbm, smem, table_sem.at[i])
        for i, (hbm, smem) in enumerate(
            ((ids_hbm, ids_ref), (src_hbm, src_ref), (count_hbm, count_ref))
        )
    ]
    for copy in tables:
        copy.start()
    for copy in tables:
        copy.wait()
    slots = ids_ref.shape[2]
    rows = own.shape[1]
    parity = lax.rem(region_ref[0], 2)
    count = count_ref[0, 0]
    for slot in range(slots):
        live = slot < count
        target = stacked.at[pl.ds(slot * rows, rows), :]
        source = src_ref[0, 0, slot]
        where = jnp.where(source == 1, 0, jnp.where((source == 2) == (parity == 0), 1, 2))
        for code, store in enumerate((own, even, odd)):

            @pl.when(live & (where == code))
            def _():
                block = store.at[ids_ref[0, 0, slot]]
                pltpu.make_async_copy(block, target, sem.at[slot]).start()

        @pl.when(jnp.logical_not(live))
        def _():
            target[...] = jnp.zeros(target.shape, target.dtype)

    for slot in range(slots):

        @pl.when(slot < count)
        def _():
            target = stacked.at[pl.ds(slot * rows, rows), :]
            pltpu.make_async_copy(own.at[0], target, sem.at[slot]).wait()

    size = gram_ref.shape[0]
    part = min(size, 256)
    for step in range(size // part):
        block = lax.dot_general(
            stacked[:, step * part : (step + 1) * part],
            stacked[...],
            (((0,), (0,)), ((), ())),
            preferred_element_type=jnp.float32,
        )
        gram_ref[step * part : (step + 1) * part, :] = (block * scale).astype(jnp.bfloat16)


def block(me_ref, j, width, rows):
    return pl.ds(pl.multiple_of((lax.div(me_ref[0], width) ^ j) * rows, rows), rows)


def within(me_ref, k, quarter, rows):
    return pl.ds(pl.multiple_of(lax.rem(me_ref[0] ^ k, quarter) * rows, rows), rows)


def early_kernel(steps, me_ref, gram_ref, *refs):
    piece_refs, (acc_ref, members_ref) = refs[:-2], refs[-2:]
    rows = piece_refs[0].shape[0]
    size = gram_ref.shape[0]
    there = block(me_ref, PARTS // 2, size // rows // PARTS, size // PARTS)
    members_ref[there, :] = jnp.zeros((size // PARTS, members_ref.shape[1]), members_ref.dtype)
    for k, piece in zip(steps, piece_refs):
        members_ref[pl.ds(pl.multiple_of((me_ref[0] ^ k) * rows, rows), rows), :] = piece[...]
    tall = size // 4
    for step in range(4):
        here = slice(step * tall, (step + 1) * tall)
        acc_ref[here, :] = jnp.dot(
            gram_ref[here, :], members_ref[...], preferred_element_type=jnp.float32
        )


def late_kernel(late_steps, out_steps, me_ref, gram_ref, acc_ref, members_ref, *refs):
    count = len(late_steps)
    late_refs, outs = refs[:count], dict(zip(out_steps, refs[count:-3]))
    first, late, fresh = refs[-3:]
    rows = late_refs[0].shape[0]
    size = gram_ref.shape[0]
    width = late.shape[0] // rows
    for k, piece in zip(late_steps, late_refs):
        late[within(me_ref, k, width, rows), :] = piece[...]
    there = block(me_ref, PARTS // 2, width, late.shape[0])
    tall = size // 4
    for step in range(4):
        here = slice(step * tall, (step + 1) * tall)
        part = jnp.dot(gram_ref[here, there], late[...], preferred_element_type=jnp.float32)
        first[here, :] = (acc_ref[here, :] + part).astype(jnp.bfloat16)
    quarter = tall // rows
    for j in (3, 2, 1, 0):
        there = block(me_ref, j, quarter, tall)
        second = jnp.dot(gram_ref[there, :], first[...], preferred_element_type=jnp.float32)
        rest = members_ref[there, :].astype(jnp.float32) - first[there, :].astype(jnp.float32)
        fresh[...] = rest + second
        for k in late_steps:
            if k // quarter == j:
                here = within(me_ref, k, quarter, rows)
                fresh[here, :] += late[within(me_ref, k, width, rows), :].astype(jnp.float32)
        for k, out_ref in outs.items():
            if k // quarter == j:
                here = within(me_ref, k, quarter, rows)
                out_ref[...] = fresh[here, :].astype(jnp.bfloat16)


def vmem():
    return pl.BlockSpec(memory_space=pltpu.VMEM)


def params():
    return pltpu.CompilerParams(vmem_limit_bytes=LIMIT)


def cost(flops, nbytes):
    return pl.CostEstimate(flops=flops, bytes_accessed=nbytes, transcendentals=0)


def swap(store, first):
    count = lax.axis_size("region")
    pairs = [(i, i + 1) for i in range(first, count - 1, 2)]
    return lax.ppermute(store, "region", pairs + [(j, i) for i, j in pairs])


def shards(ensemble, obs_store, block_ids, block_src, block_count):
    rows, _, patches, values = ensemble.shape
    store = obs_store.reshape(obs_store.shape[2:])
    size = store.shape[2]
    slots = block_ids.shape[2]
    me = lax.axis_index("member").astype(jnp.int32).reshape(1)
    region = lax.axis_index("region").astype(jnp.int32).reshape(1)
    smem = pl.BlockSpec(memory_space=pltpu.SMEM)
    hbm = pl.BlockSpec(memory_space=pltpu.HBM)
    piece_shape = jax.ShapeDtypeStruct((rows, values), jnp.bfloat16)

    odd, even = swap(store, 1), swap(store, 0)
    steps = [0] + inward(patches)
    pieces = pl.pallas_call(
        functools.partial(split_kernel, steps),
        out_shape=[piece_shape] * patches,
        in_specs=[smem, vmem()],
        out_specs=[vmem()] * patches,
        compiler_params=params(),
        cost_estimate=cost(2 * 256 * rows * patches * values, 4 * rows * patches * values),
        name="split",
    )(me, ensemble.reshape(rows * patches, values))
    arrived = {k: ppermute(piece, "member", k) for k, piece in zip(steps, pieces)}

    gram = pl.pallas_call(
        functools.partial(gram_kernel, 1.0 / (2.0 * size)),
        out_shape=jax.ShapeDtypeStruct((size, size), jnp.bfloat16),
        in_specs=[smem] + [hbm] * 6,
        out_specs=vmem(),
        scratch_shapes=[
            pltpu.SMEM(block_ids.shape, jnp.int32),
            pltpu.SMEM(block_src.shape, jnp.int32),
            pltpu.SMEM(block_count.shape, jnp.int32),
            pltpu.VMEM((slots * store.shape[1], size), jnp.bfloat16),
            pltpu.SemaphoreType.DMA((3,)),
            pltpu.SemaphoreType.DMA((slots,)),
        ],
        compiler_params=params(),
        cost_estimate=cost(2 * slots * store.shape[1] * size * size, 4 * size * size),
        name="gram",
    )(region, block_ids, block_src, block_count, store, even, odd)

    early = [k for k in steps if not is_late(k, patches)]
    late = [k for k in steps if is_late(k, patches)]
    matrix = jax.ShapeDtypeStruct((size, values), jnp.bfloat16)
    acc, members = pl.pallas_call(
        functools.partial(early_kernel, early),
        out_shape=[jax.ShapeDtypeStruct((size, values), jnp.float32), matrix],
        in_specs=[smem] + [vmem()] * (1 + len(early)),
        out_specs=[vmem()] * 2,
        compiler_params=params(),
        cost_estimate=cost(2 * size * size * values, 2 * size * size + 8 * size * values),
        name="early",
    )(me, gram, *[arrived[k] for k in early])
    back = partners(patches) + [0]
    moved = pl.pallas_call(
        functools.partial(late_kernel, late, back),
        out_shape=[piece_shape] * patches,
        in_specs=[smem] + [vmem()] * (3 + len(late)),
        out_specs=[vmem()] * patches,
        scratch_shapes=[
            pltpu.VMEM((size, values), jnp.bfloat16),
            pltpu.VMEM((size // PARTS, values), jnp.bfloat16),
            pltpu.VMEM((size // 4, values), jnp.float32),
        ],
        compiler_params=params(),
        cost_estimate=cost(3 * size * size * values, 2 * size * size + 10 * size * values),
        name="late",
    )(me, gram, acc, members, *[arrived[k] for k in late])
    order = back
    returned = [ppermute(piece, "member", k) for k, piece in zip(back, moved)]

    fresh = pl.pallas_call(
        functools.partial(merge_kernel, order),
        out_shape=jax.ShapeDtypeStruct((rows * patches, values), jnp.bfloat16),
        in_specs=[smem] + [vmem()] * patches,
        out_specs=vmem(),
        compiler_params=params(),
        cost_estimate=cost(2 * 256 * rows * patches * values, 4 * rows * patches * values),
        name="merge",
    )(me, *returned)
    return fresh.reshape(ensemble.shape)


def solution(mesh):
    return jax.shard_map(
        shards,
        mesh=mesh,
        in_specs=(
            P("member", "region", None, None),
            P("region", "member", None, None, None),
            P("region", "member", None),
            P("region", "member", None),
            P("region", "member"),
        ),
        out_specs=P("member", "region", None, None),
        check_vma=False,
    )
```

```python
import functools

import jax
import jax.numpy as jnp
from jax import lax
from jax.experimental import pallas as pl
from jax.experimental.pallas import tpu as pltpu
from jax.sharding import PartitionSpec as P

LIMIT = 16 * 1024 * 1024


def rows_per_group(rows, patches):
    return min(rows, max(16, 256 // patches))


PARTS = 4


def is_late(k, count):
    return k // (count // PARTS) == PARTS // 2


def partners(count):
    far = list(range(count - 1, count // 2 - 1, -1))
    near = list(range(count // 2 - 1, 0, -1))
    order = []
    for i in range(len(far)):
        order += far[i : i + 1] + near[i : i + 1]
    return order


def inward(count):
    order = partners(count)
    return [k for k in order if not is_late(k, count)] + [k for k in order if is_late(k, count)]


def ppermute(value, axis, step):
    if step == 0:
        return value
    count = lax.axis_size(axis)
    return lax.ppermute(value, axis, [(i, i ^ step) for i in range(count)])


def split_kernel(steps, me_ref, members_ref, *out_refs):
    patches = len(steps)
    rows = out_refs[0].shape[0]
    group = rows_per_group(rows, patches)
    height = group * patches
    row = lax.broadcasted_iota(jnp.int32, (height, height), 0)
    column = lax.broadcasted_iota(jnp.int32, (height, height), 1)
    source = lax.rem(row, group) * patches + (lax.div(row, group) ^ me_ref[0])
    shuffle = jnp.where(column == source, 1.0, 0.0).astype(jnp.bfloat16)
    for step in range(rows // group):
        block = members_ref[step * height : (step + 1) * height, :]
        moved = jnp.dot(shuffle, block, preferred_element_type=jnp.float32)
        moved = moved.astype(jnp.bfloat16)
        for k, out_ref in zip(steps, out_refs):
            out_ref[step * group : (step + 1) * group, :] = moved[k * group : (k + 1) * group, :]


def merge_kernel(order, me_ref, *refs):
    patches = len(order)
    piece_refs, (out_ref, whole, sem) = dict(zip(order, refs)), refs[patches:]
    rows = piece_refs[0].shape[0]
    group = rows_per_group(rows, patches)
    height = group * patches
    row = lax.broadcasted_iota(jnp.int32, (height, height), 0)
    column = lax.broadcasted_iota(jnp.int32, (height, height), 1)
    source = (lax.rem(row, patches) ^ me_ref[0]) * group + lax.div(row, patches)
    shuffle = jnp.where(column == source, 1.0, 0.0).astype(jnp.bfloat16)
    copies = []
    for step in range(rows // group):
        here = slice(step * group, (step + 1) * group)
        block = jnp.concatenate([piece_refs[k][here, :] for k in range(patches)], axis=0)
        moved = jnp.dot(shuffle, block, preferred_element_type=jnp.float32)
        there = pl.ds(step * height, height)
        whole[there, :] = moved.astype(jnp.bfloat16)
        copies.append(pltpu.make_async_copy(whole.at[there, :], out_ref.at[there, :], sem.at[step]))
        copies[-1].start()
    for copy in copies:
        copy.wait()


def gram_kernel(
    scale, region_ref, ids_hbm, src_hbm, count_hbm, own, even, odd, gram_ref,
    ids_ref, src_ref, count_ref, stacked, table_sem, sem,
):
    tables = [
        pltpu.make_async_copy(hbm, smem, table_sem.at[i])
        for i, (hbm, smem) in enumerate(
            ((ids_hbm, ids_ref), (src_hbm, src_ref), (count_hbm, count_ref))
        )
    ]
    for copy in tables:
        copy.start()
    for copy in tables:
        copy.wait()
    slots = ids_ref.shape[2]
    rows = own.shape[1]
    parity = lax.rem(region_ref[0], 2)
    count = count_ref[0, 0]
    for slot in range(slots):
        live = slot < count
        target = stacked.at[pl.ds(slot * rows, rows), :]
        source = src_ref[0, 0, slot]
        where = jnp.where(source == 1, 0, jnp.where((source == 2) == (parity == 0), 1, 2))
        for code, store in enumerate((own, even, odd)):

            @pl.when(live & (where == code))
            def _():
                block = store.at[ids_ref[0, 0, slot]]
                pltpu.make_async_copy(block, target, sem.at[slot]).start()

        @pl.when(jnp.logical_not(live))
        def _():
            target[...] = jnp.zeros(target.shape, target.dtype)

    for slot in range(slots):

        @pl.when(slot < count)
        def _():
            target = stacked.at[pl.ds(slot * rows, rows), :]
            pltpu.make_async_copy(own.at[0], target, sem.at[slot]).wait()

    size = gram_ref.shape[0]
    part = min(size, 256)
    for step in range(size // part):
        block = lax.dot_general(
            stacked[:, step * part : (step + 1) * part],
            stacked[...],
            (((0,), (0,)), ((), ())),
            preferred_element_type=jnp.float32,
        )
        gram_ref[step * part : (step + 1) * part, :] = (block * scale).astype(jnp.bfloat16)


def block(me_ref, j, width, rows):
    return pl.ds(pl.multiple_of((lax.div(me_ref[0], width) ^ j) * rows, rows), rows)


def within(me_ref, k, quarter, rows):
    return pl.ds(pl.multiple_of(lax.rem(me_ref[0] ^ k, quarter) * rows, rows), rows)


def early_kernel(steps, me_ref, gram_ref, *refs):
    piece_refs, (acc_ref, members_ref) = refs[:-2], refs[-2:]
    rows = piece_refs[0].shape[0]
    size = gram_ref.shape[0]
    there = block(me_ref, PARTS // 2, size // rows // PARTS, size // PARTS)
    members_ref[there, :] = jnp.zeros((size // PARTS, members_ref.shape[1]), members_ref.dtype)
    for k, piece in zip(steps, piece_refs):
        members_ref[pl.ds(pl.multiple_of((me_ref[0] ^ k) * rows, rows), rows), :] = piece[...]
    tall = size // 4
    for step in range(4):
        here = slice(step * tall, (step + 1) * tall)
        acc_ref[here, :] = jnp.dot(
            gram_ref[here, :], members_ref[...], preferred_element_type=jnp.float32
        )


def late_kernel(late_steps, out_steps, me_ref, gram_ref, acc_ref, members_ref, *refs):
    count = len(late_steps)
    late_refs, outs = refs[:count], dict(zip(out_steps, refs[count:-3]))
    first, late, fresh = refs[-3:]
    rows = late_refs[0].shape[0]
    size = gram_ref.shape[0]
    width = late.shape[0] // rows
    for k, piece in zip(late_steps, late_refs):
        late[within(me_ref, k, width, rows), :] = piece[...]
    there = block(me_ref, PARTS // 2, width, late.shape[0])
    tall = size // 4
    for step in range(4):
        here = slice(step * tall, (step + 1) * tall)
        part = jnp.dot(gram_ref[here, there], late[...], preferred_element_type=jnp.float32)
        first[here, :] = (acc_ref[here, :] + part).astype(jnp.bfloat16)
    quarter = tall // rows
    for j in (3, 2, 1, 0):
        there = block(me_ref, j, quarter, tall)
        second = jnp.dot(gram_ref[there, :], first[...], preferred_element_type=jnp.float32)
        rest = members_ref[there, :].astype(jnp.float32) - first[there, :].astype(jnp.float32)
        fresh[...] = rest + second
        for k in late_steps:
            if k // quarter == j:
                here = within(me_ref, k, quarter, rows)
                fresh[here, :] += late[within(me_ref, k, width, rows), :].astype(jnp.float32)
        for k, out_ref in outs.items():
            if k // quarter == j:
                here = within(me_ref, k, quarter, rows)
                out_ref[...] = fresh[here, :].astype(jnp.bfloat16)


def vmem():
    return pl.BlockSpec(memory_space=pltpu.VMEM)


def params():
    return pltpu.CompilerParams(vmem_limit_bytes=LIMIT)


def cost(flops, nbytes):
    return pl.CostEstimate(flops=flops, bytes_accessed=nbytes, transcendentals=0)


def swap(store, first):
    count = lax.axis_size("region")
    pairs = [(i, i + 1) for i in range(first, count - 1, 2)]
    return lax.ppermute(store, "region", pairs + [(j, i) for i, j in pairs])


def shards(ensemble, obs_store, block_ids, block_src, block_count):
    rows, _, patches, values = ensemble.shape
    store = obs_store.reshape(obs_store.shape[2:])
    size = store.shape[2]
    slots = block_ids.shape[2]
    me = lax.axis_index("member").astype(jnp.int32).reshape(1)
    region = lax.axis_index("region").astype(jnp.int32).reshape(1)
    smem = pl.BlockSpec(memory_space=pltpu.SMEM)
    hbm = pl.BlockSpec(memory_space=pltpu.HBM)
    piece_shape = jax.ShapeDtypeStruct((rows, values), jnp.bfloat16)

    odd, even = swap(store, 1), swap(store, 0)
    steps = [0] + inward(patches)
    pieces = pl.pallas_call(
        functools.partial(split_kernel, steps),
        out_shape=[piece_shape] * patches,
        in_specs=[smem, vmem()],
        out_specs=[vmem()] * patches,
        compiler_params=params(),
        cost_estimate=cost(2 * 256 * rows * patches * values, 4 * rows * patches * values),
        name="split",
    )(me, ensemble.reshape(rows * patches, values))
    arrived = {k: ppermute(piece, "member", k) for k, piece in zip(steps, pieces)}

    gram = pl.pallas_call(
        functools.partial(gram_kernel, 1.0 / (2.0 * size)),
        out_shape=jax.ShapeDtypeStruct((size, size), jnp.bfloat16),
        in_specs=[smem] + [hbm] * 6,
        out_specs=vmem(),
        scratch_shapes=[
            pltpu.SMEM(block_ids.shape, jnp.int32),
            pltpu.SMEM(block_src.shape, jnp.int32),
            pltpu.SMEM(block_count.shape, jnp.int32),
            pltpu.VMEM((slots * store.shape[1], size), jnp.bfloat16),
            pltpu.SemaphoreType.DMA((3,)),
            pltpu.SemaphoreType.DMA((slots,)),
        ],
        compiler_params=params(),
        cost_estimate=cost(2 * slots * store.shape[1] * size * size, 4 * size * size),
        name="gram",
    )(region, block_ids, block_src, block_count, store, even, odd)

    early = [k for k in steps if not is_late(k, patches)]
    late = [k for k in steps if is_late(k, patches)]
    matrix = jax.ShapeDtypeStruct((size, values), jnp.bfloat16)
    acc, members = pl.pallas_call(
        functools.partial(early_kernel, early),
        out_shape=[jax.ShapeDtypeStruct((size, values), jnp.float32), matrix],
        in_specs=[smem] + [vmem()] * (1 + len(early)),
        out_specs=[vmem()] * 2,
        compiler_params=params(),
        cost_estimate=cost(2 * size * size * values, 2 * size * size + 8 * size * values),
        name="early",
    )(me, gram, *[arrived[k] for k in early])
    back = partners(patches) + [0]
    moved = pl.pallas_call(
        functools.partial(late_kernel, late, back),
        out_shape=[piece_shape] * patches,
        in_specs=[smem] + [vmem()] * (3 + len(late)),
        out_specs=[vmem()] * patches,
        scratch_shapes=[
            pltpu.VMEM((size, values), jnp.bfloat16),
            pltpu.VMEM((size // PARTS, values), jnp.bfloat16),
            pltpu.VMEM((size // 4, values), jnp.float32),
        ],
        compiler_params=params(),
        cost_estimate=cost(3 * size * size * values, 2 * size * size + 10 * size * values),
        name="late",
    )(me, gram, acc, members, *[arrived[k] for k in late])
    order = back
    returned = [ppermute(piece, "member", k) for k, piece in zip(back, moved)]

    steps = rows // rows_per_group(rows, patches)
    fresh = pl.pallas_call(
        functools.partial(merge_kernel, order),
        out_shape=jax.ShapeDtypeStruct((rows * patches, values), jnp.bfloat16),
        in_specs=[smem] + [vmem()] * patches,
        out_specs=pl.BlockSpec(memory_space=pl.ANY),
        scratch_shapes=[
            pltpu.VMEM((rows * patches, values), jnp.bfloat16),
            pltpu.SemaphoreType.DMA((steps,)),
        ],
        compiler_params=params(),
        cost_estimate=cost(2 * 256 * rows * patches * values, 4 * rows * patches * values),
        name="merge",
    )(me, *returned)
    return fresh.reshape(ensemble.shape)


def solution(mesh):
    return jax.shard_map(
        shards,
        mesh=mesh,
        in_specs=(
            P("member", "region", None, None),
            P("region", "member", None, None, None),
            P("region", "member", None),
            P("region", "member", None),
            P("region", "member"),
        ),
        out_specs=P("member", "region", None, None),
        check_vma=False,
    )
```

```python
import functools

import jax
import jax.numpy as jnp
from jax import lax
from jax.experimental import pallas as pl
from jax.experimental.pallas import tpu as pltpu
from jax.sharding import PartitionSpec as P

LIMIT = 16 * 1024 * 1024


def rows_per_group(rows, patches):
    return min(rows, max(16, 256 // patches))


PARTS = 4


def is_late(k, count):
    return k // (count // PARTS) == PARTS // 2


def partners(count):
    far = list(range(count - 1, count // 2 - 1, -1))
    near = list(range(count // 2 - 1, 0, -1))
    order = []
    for i in range(len(far)):
        order += far[i : i + 1] + near[i : i + 1]
    return order


def inward(count):
    order = partners(count)
    return [k for k in order if not is_late(k, count)] + [k for k in order if is_late(k, count)]


def ppermute(value, axis, step):
    if step == 0:
        return value
    count = lax.axis_size(axis)
    return lax.ppermute(value, axis, [(i, i ^ step) for i in range(count)])


def split_kernel(steps, me_ref, members_ref, *out_refs):
    patches = len(steps)
    rows = out_refs[0].shape[0]
    group = rows_per_group(rows, patches)
    height = group * patches
    row = lax.broadcasted_iota(jnp.int32, (height, height), 0)
    column = lax.broadcasted_iota(jnp.int32, (height, height), 1)
    source = lax.rem(row, group) * patches + (lax.div(row, group) ^ me_ref[0])
    shuffle = jnp.where(column == source, 1.0, 0.0).astype(jnp.bfloat16)
    for step in range(rows // group):
        block = members_ref[step * height : (step + 1) * height, :]
        moved = jnp.dot(shuffle, block, preferred_element_type=jnp.float32)
        moved = moved.astype(jnp.bfloat16)
        for k, out_ref in zip(steps, out_refs):
            out_ref[step * group : (step + 1) * group, :] = moved[k * group : (k + 1) * group, :]


def merge_kernel(order, me_ref, *refs):
    patches = len(order)
    piece_refs, (out_ref, whole, sem) = dict(zip(order, refs)), refs[patches:]
    rows = piece_refs[0].shape[0]
    group = rows_per_group(rows, patches)
    height = group * patches
    row = lax.broadcasted_iota(jnp.int32, (height, height), 0)
    column = lax.broadcasted_iota(jnp.int32, (height, height), 1)
    source = (lax.rem(row, patches) ^ me_ref[0]) * group + lax.div(row, patches)
    shuffle = jnp.where(column == source, 1.0, 0.0).astype(jnp.bfloat16)
    copies = []
    for step in range(rows // group):
        here = slice(step * group, (step + 1) * group)
        block = jnp.concatenate([piece_refs[k][here, :] for k in range(patches)], axis=0)
        moved = jnp.dot(shuffle, block, preferred_element_type=jnp.float32)
        there = pl.ds(step * height, height)
        whole[there, :] = moved.astype(jnp.bfloat16)
        copies.append(pltpu.make_async_copy(whole.at[there, :], out_ref.at[there, :], sem.at[step]))
        copies[-1].start()
    for copy in copies:
        copy.wait()


def gram_kernel(scale, region_ref, table_ref, both, odd, gram_ref, stacked, sem):
    slots = (table_ref.shape[0] - 1) // 2
    rows = odd.shape[1]
    parity = lax.rem(region_ref[0], 2)
    count = table_ref[2 * slots]
    for slot in range(slots):
        live = slot < count
        target = stacked.at[pl.ds(slot * rows, rows), :]
        index, source = table_ref[slot], table_ref[slots + slot]
        swapped = (source != 1) & ((source == 2) != (parity == 0))
        member = jnp.where(source == 1, parity, 1 - parity)

        @pl.when(live & jnp.logical_not(swapped))
        def _():
            pltpu.make_async_copy(both.at[member, index], target, sem.at[slot]).start()

        @pl.when(live & swapped)
        def _():
            pltpu.make_async_copy(odd.at[index], target, sem.at[slot]).start()

        @pl.when(jnp.logical_not(live))
        def _():
            target[...] = jnp.zeros(target.shape, target.dtype)

    for slot in range(slots):

        @pl.when(slot < count)
        def _():
            target = stacked.at[pl.ds(slot * rows, rows), :]
            pltpu.make_async_copy(odd.at[0], target, sem.at[slot]).wait()

    size = gram_ref.shape[0]
    part = min(size, 256)
    for step in range(size // part):
        block = lax.dot_general(
            stacked[:, step * part : (step + 1) * part],
            stacked[...],
            (((0,), (0,)), ((), ())),
            preferred_element_type=jnp.float32,
        )
        gram_ref[step * part : (step + 1) * part, :] = (block * scale).astype(jnp.bfloat16)


def block(me_ref, j, width, rows):
    return pl.ds(pl.multiple_of((lax.div(me_ref[0], width) ^ j) * rows, rows), rows)


def within(me_ref, k, quarter, rows):
    return pl.ds(pl.multiple_of(lax.rem(me_ref[0] ^ k, quarter) * rows, rows), rows)


def early_kernel(steps, me_ref, gram_ref, *refs):
    piece_refs, (acc_ref, members_ref) = refs[:-2], refs[-2:]
    rows = piece_refs[0].shape[0]
    size = gram_ref.shape[0]
    there = block(me_ref, PARTS // 2, size // rows // PARTS, size // PARTS)
    members_ref[there, :] = jnp.zeros((size // PARTS, members_ref.shape[1]), members_ref.dtype)
    for k, piece in zip(steps, piece_refs):
        members_ref[pl.ds(pl.multiple_of((me_ref[0] ^ k) * rows, rows), rows), :] = piece[...]
    tall = size // 4
    for step in range(4):
        here = slice(step * tall, (step + 1) * tall)
        acc_ref[here, :] = jnp.dot(
            gram_ref[here, :], members_ref[...], preferred_element_type=jnp.float32
        )


def late_kernel(late_steps, out_steps, me_ref, gram_ref, acc_ref, members_ref, *refs):
    count = len(late_steps)
    late_refs, outs = refs[:count], dict(zip(out_steps, refs[count:-3]))
    first, late, fresh = refs[-3:]
    rows = late_refs[0].shape[0]
    size = gram_ref.shape[0]
    width = late.shape[0] // rows
    for k, piece in zip(late_steps, late_refs):
        late[within(me_ref, k, width, rows), :] = piece[...]
    there = block(me_ref, PARTS // 2, width, late.shape[0])
    tall = size // 4
    for step in range(4):
        here = slice(step * tall, (step + 1) * tall)
        part = jnp.dot(gram_ref[here, there], late[...], preferred_element_type=jnp.float32)
        first[here, :] = (acc_ref[here, :] + part).astype(jnp.bfloat16)
    quarter = tall // rows
    for j in (3, 2, 1, 0):
        there = block(me_ref, j, quarter, tall)
        second = jnp.dot(gram_ref[there, :], first[...], preferred_element_type=jnp.float32)
        rest = members_ref[there, :].astype(jnp.float32) - first[there, :].astype(jnp.float32)
        fresh[...] = rest + second
        for k in late_steps:
            if k // quarter == j:
                here = within(me_ref, k, quarter, rows)
                fresh[here, :] += late[within(me_ref, k, width, rows), :].astype(jnp.float32)
        for k, out_ref in outs.items():
            if k // quarter == j:
                here = within(me_ref, k, quarter, rows)
                out_ref[...] = fresh[here, :].astype(jnp.bfloat16)


def vmem():
    return pl.BlockSpec(memory_space=pltpu.VMEM)


def params():
    return pltpu.CompilerParams(vmem_limit_bytes=LIMIT)


def cost(flops, nbytes):
    return pl.CostEstimate(flops=flops, bytes_accessed=nbytes, transcendentals=0)


def halo(store):
    count = lax.axis_size("region")
    groups = [[i, i + 1] for i in range(0, count, 2)]
    both = lax.all_gather(store, "region", axis_index_groups=groups)
    pairs = [(i, i + 1) for i in range(1, count - 1, 2)]
    return both, lax.ppermute(store, "region", pairs + [(j, i) for i, j in pairs])


def shards(ensemble, obs_store, block_ids, block_src, block_count):
    rows, _, patches, values = ensemble.shape
    store = obs_store.reshape(obs_store.shape[2:])
    size = store.shape[2]
    slots = block_ids.shape[2]
    me = lax.axis_index("member").astype(jnp.int32).reshape(1)
    region = lax.axis_index("region").astype(jnp.int32).reshape(1)
    smem = pl.BlockSpec(memory_space=pltpu.SMEM)
    hbm = pl.BlockSpec(memory_space=pltpu.HBM)
    piece_shape = jax.ShapeDtypeStruct((rows, values), jnp.bfloat16)

    both, odd = halo(store)
    steps = [0] + inward(patches)
    pieces = pl.pallas_call(
        functools.partial(split_kernel, steps),
        out_shape=[piece_shape] * patches,
        in_specs=[smem, vmem()],
        out_specs=[vmem()] * patches,
        compiler_params=params(),
        cost_estimate=cost(2 * 256 * rows * patches * values, 4 * rows * patches * values),
        name="split",
    )(me, ensemble.reshape(rows * patches, values))
    arrived = {k: ppermute(piece, "member", k) for k, piece in zip(steps, pieces)}

    table = jnp.concatenate([block_ids.ravel(), block_src.ravel(), block_count.ravel()])
    gram = pl.pallas_call(
        functools.partial(gram_kernel, 1.0 / (2.0 * size)),
        out_shape=jax.ShapeDtypeStruct((size, size), jnp.bfloat16),
        in_specs=[smem] * 2 + [hbm] * 2,
        out_specs=vmem(),
        scratch_shapes=[
            pltpu.VMEM((slots * store.shape[1], size), jnp.bfloat16),
            pltpu.SemaphoreType.DMA((slots,)),
        ],
        compiler_params=params(),
        cost_estimate=cost(2 * slots * store.shape[1] * size * size, 4 * size * size),
        name="gram",
    )(region, table, both, odd)

    early = [k for k in steps if not is_late(k, patches)]
    late = [k for k in steps if is_late(k, patches)]
    matrix = jax.ShapeDtypeStruct((size, values), jnp.bfloat16)
    acc, members = pl.pallas_call(
        functools.partial(early_kernel, early),
        out_shape=[jax.ShapeDtypeStruct((size, values), jnp.float32), matrix],
        in_specs=[smem] + [vmem()] * (1 + len(early)),
        out_specs=[vmem()] * 2,
        compiler_params=params(),
        cost_estimate=cost(2 * size * size * values, 2 * size * size + 8 * size * values),
        name="early",
    )(me, gram, *[arrived[k] for k in early])
    back = partners(patches) + [0]
    moved = pl.pallas_call(
        functools.partial(late_kernel, late, back),
        out_shape=[piece_shape] * patches,
        in_specs=[smem] + [vmem()] * (3 + len(late)),
        out_specs=[vmem()] * patches,
        scratch_shapes=[
            pltpu.VMEM((size, values), jnp.bfloat16),
            pltpu.VMEM((size // PARTS, values), jnp.bfloat16),
            pltpu.VMEM((size // 4, values), jnp.float32),
        ],
        compiler_params=params(),
        cost_estimate=cost(3 * size * size * values, 2 * size * size + 10 * size * values),
        name="late",
    )(me, gram, acc, members, *[arrived[k] for k in late])
    order = back
    returned = [ppermute(piece, "member", k) for k, piece in zip(back, moved)]

    steps = rows // rows_per_group(rows, patches)
    fresh = pl.pallas_call(
        functools.partial(merge_kernel, order),
        out_shape=jax.ShapeDtypeStruct((rows * patches, values), jnp.bfloat16),
        in_specs=[smem] + [vmem()] * patches,
        out_specs=pl.BlockSpec(memory_space=pl.ANY),
        scratch_shapes=[
            pltpu.VMEM((rows * patches, values), jnp.bfloat16),
            pltpu.SemaphoreType.DMA((steps,)),
        ],
        compiler_params=params(),
        cost_estimate=cost(2 * 256 * rows * patches * values, 4 * rows * patches * values),
        name="merge",
    )(me, *returned)
    return fresh.reshape(ensemble.shape)


def solution(mesh):
    return jax.shard_map(
        shards,
        mesh=mesh,
        in_specs=(
            P("member", "region", None, None),
            P("region", "member", None, None, None),
            P("region", "member", None),
            P("region", "member", None),
            P("region", "member"),
        ),
        out_specs=P("member", "region", None, None),
        check_vma=False,
    )
```

```python
import functools

import jax
import jax.numpy as jnp
from jax import lax
from jax.experimental import pallas as pl
from jax.experimental.pallas import tpu as pltpu
from jax.sharding import PartitionSpec as P

LIMIT = 16 * 1024 * 1024


def rows_per_group(rows, patches):
    return min(rows, max(16, 256 // patches))


PARTS = 8


def is_late(k, count):
    return k // (count // PARTS) == PARTS // 2


def partners(count):
    far = list(range(count - 1, count // 2 - 1, -1))
    near = list(range(count // 2 - 1, 0, -1))
    order = []
    for i in range(len(far)):
        order += far[i : i + 1] + near[i : i + 1]
    return order


def inward(count):
    order = [k for k in partners(count) if not is_late(k, count)]
    last_far = order.index(min(k for k in order if k >= count // 2))
    order.insert(min(3, last_far), order.pop(last_far))
    return order + [k for k in partners(count) if is_late(k, count)]


def ppermute(value, axis, step):
    if step == 0:
        return value
    count = lax.axis_size(axis)
    return lax.ppermute(value, axis, [(i, i ^ step) for i in range(count)])


def split_kernel(steps, me_ref, members_ref, *out_refs):
    patches = len(steps)
    rows = out_refs[0].shape[0]
    group = rows_per_group(rows, patches)
    height = group * patches
    row = lax.broadcasted_iota(jnp.int32, (height, height), 0)
    column = lax.broadcasted_iota(jnp.int32, (height, height), 1)
    source = lax.rem(row, group) * patches + (lax.div(row, group) ^ me_ref[0])
    shuffle = jnp.where(column == source, 1.0, 0.0).astype(jnp.bfloat16)
    for step in range(rows // group):
        block = members_ref[step * height : (step + 1) * height, :]
        moved = jnp.dot(shuffle, block, preferred_element_type=jnp.float32)
        moved = moved.astype(jnp.bfloat16)
        for k, out_ref in zip(steps, out_refs):
            out_ref[step * group : (step + 1) * group, :] = moved[k * group : (k + 1) * group, :]


def merge_kernel(order, me_ref, *refs):
    patches = len(order)
    piece_refs, (out_ref, whole, sem) = dict(zip(order, refs)), refs[patches:]
    rows = piece_refs[0].shape[0]
    group = rows_per_group(rows, patches)
    height = group * patches
    row = lax.broadcasted_iota(jnp.int32, (height, height), 0)
    column = lax.broadcasted_iota(jnp.int32, (height, height), 1)
    source = (lax.rem(row, patches) ^ me_ref[0]) * group + lax.div(row, patches)
    shuffle = jnp.where(column == source, 1.0, 0.0).astype(jnp.bfloat16)
    copies = []
    for step in range(rows // group):
        here = slice(step * group, (step + 1) * group)
        block = jnp.concatenate([piece_refs[k][here, :] for k in range(patches)], axis=0)
        moved = jnp.dot(shuffle, block, preferred_element_type=jnp.float32)
        there = pl.ds(step * height, height)
        whole[there, :] = moved.astype(jnp.bfloat16)
        copies.append(pltpu.make_async_copy(whole.at[there, :], out_ref.at[there, :], sem.at[step]))
        copies[-1].start()
    for copy in copies:
        copy.wait()


def gram_kernel(scale, region_ref, table_ref, own, even, odd, gram_ref, stacked, sem):
    slots = (table_ref.shape[0] - 1) // 2
    rows = own.shape[1]
    parity = lax.rem(region_ref[0], 2)
    count = table_ref[2 * slots]
    for slot in range(slots):
        live = slot < count
        target = stacked.at[pl.ds(slot * rows, rows), :]
        index, source = table_ref[slot], table_ref[slots + slot]
        where = jnp.where(source == 1, 0, jnp.where((source == 2) == (parity == 0), 1, 2))
        for code, store in enumerate((own, even, odd)):

            @pl.when(live & (where == code))
            def _():
                pltpu.make_async_copy(store.at[index], target, sem.at[slot]).start()

        @pl.when(jnp.logical_not(live))
        def _():
            target[...] = jnp.zeros(target.shape, target.dtype)

    for slot in range(slots):

        @pl.when(slot < count)
        def _():
            target = stacked.at[pl.ds(slot * rows, rows), :]
            pltpu.make_async_copy(odd.at[0], target, sem.at[slot]).wait()

    size = gram_ref.shape[0]
    part = min(size, 256)
    for step in range(size // part):
        block = lax.dot_general(
            stacked[:, step * part : (step + 1) * part],
            stacked[...],
            (((0,), (0,)), ((), ())),
            preferred_element_type=jnp.float32,
        )
        gram_ref[step * part : (step + 1) * part, :] = (block * scale).astype(jnp.bfloat16)


def block(me_ref, j, width, rows):
    return pl.ds(pl.multiple_of((lax.div(me_ref[0], width) ^ j) * rows, rows), rows)


def within(me_ref, k, quarter, rows):
    return pl.ds(pl.multiple_of(lax.rem(me_ref[0] ^ k, quarter) * rows, rows), rows)


def early_kernel(steps, me_ref, gram_ref, *refs):
    piece_refs, (acc_ref, members_ref) = refs[:-2], refs[-2:]
    rows = piece_refs[0].shape[0]
    size = gram_ref.shape[0]
    there = block(me_ref, PARTS // 2, size // rows // PARTS, size // PARTS)
    members_ref[there, :] = jnp.zeros((size // PARTS, members_ref.shape[1]), members_ref.dtype)
    for k, piece in zip(steps, piece_refs):
        members_ref[pl.ds(pl.multiple_of((me_ref[0] ^ k) * rows, rows), rows), :] = piece[...]
    tall = size // 4
    for step in range(4):
        here = slice(step * tall, (step + 1) * tall)
        acc_ref[here, :] = jnp.dot(
            gram_ref[here, :], members_ref[...], preferred_element_type=jnp.float32
        )


def late_kernel(late_steps, out_steps, me_ref, gram_ref, acc_ref, members_ref, *refs):
    count = len(late_steps)
    late_refs, outs = refs[:count], dict(zip(out_steps, refs[count:-3]))
    first, late, fresh = refs[-3:]
    rows = late_refs[0].shape[0]
    size = gram_ref.shape[0]
    width = late.shape[0] // rows
    for k, piece in zip(late_steps, late_refs):
        late[within(me_ref, k, width, rows), :] = piece[...]
    there = block(me_ref, PARTS // 2, width, late.shape[0])
    tall = size // 4
    for step in range(4):
        here = slice(step * tall, (step + 1) * tall)
        part = jnp.dot(gram_ref[here, there], late[...], preferred_element_type=jnp.float32)
        first[here, :] = (acc_ref[here, :] + part).astype(jnp.bfloat16)
    quarter = tall // rows
    for j in (3, 2, 1, 0):
        there = block(me_ref, j, quarter, tall)
        second = jnp.dot(gram_ref[there, :], first[...], preferred_element_type=jnp.float32)
        rest = members_ref[there, :].astype(jnp.float32) - first[there, :].astype(jnp.float32)
        fresh[...] = rest + second
        for k in late_steps:
            if k // quarter == j:
                here = within(me_ref, k, quarter, rows)
                fresh[here, :] += late[within(me_ref, k, width, rows), :].astype(jnp.float32)
        for k, out_ref in outs.items():
            if k // quarter == j:
                here = within(me_ref, k, quarter, rows)
                out_ref[...] = fresh[here, :].astype(jnp.bfloat16)


def vmem():
    return pl.BlockSpec(memory_space=pltpu.VMEM)


def params():
    return pltpu.CompilerParams(vmem_limit_bytes=LIMIT)


def cost(flops, nbytes):
    return pl.CostEstimate(flops=flops, bytes_accessed=nbytes, transcendentals=0)


def swap(store, first):
    count = lax.axis_size("region")
    pairs = [(i, i + 1) for i in range(first, count - 1, 2)]
    return lax.ppermute(store, "region", pairs + [(j, i) for i, j in pairs])


def shards(ensemble, obs_store, block_ids, block_src, block_count):
    rows, _, patches, values = ensemble.shape
    store = obs_store.reshape(obs_store.shape[2:])
    size = store.shape[2]
    slots = block_ids.shape[2]
    me = lax.axis_index("member").astype(jnp.int32).reshape(1)
    region = lax.axis_index("region").astype(jnp.int32).reshape(1)
    smem = pl.BlockSpec(memory_space=pltpu.SMEM)
    hbm = pl.BlockSpec(memory_space=pltpu.HBM)
    piece_shape = jax.ShapeDtypeStruct((rows, values), jnp.bfloat16)

    odd, even = swap(store, 1), swap(store, 0)
    steps = [0] + inward(patches)
    pieces = pl.pallas_call(
        functools.partial(split_kernel, steps),
        out_shape=[piece_shape] * patches,
        in_specs=[smem, vmem()],
        out_specs=[vmem()] * patches,
        compiler_params=params(),
        cost_estimate=cost(2 * 256 * rows * patches * values, 4 * rows * patches * values),
        name="split",
    )(me, ensemble.reshape(rows * patches, values))
    arrived = {k: ppermute(piece, "member", k) for k, piece in zip(steps, pieces)}

    table = jnp.concatenate([block_ids.ravel(), block_src.ravel(), block_count.ravel()])
    gram = pl.pallas_call(
        functools.partial(gram_kernel, 1.0 / (2.0 * size)),
        out_shape=jax.ShapeDtypeStruct((size, size), jnp.bfloat16),
        in_specs=[smem] * 2 + [hbm] * 3,
        out_specs=vmem(),
        scratch_shapes=[
            pltpu.VMEM((slots * store.shape[1], size), jnp.bfloat16),
            pltpu.SemaphoreType.DMA((slots,)),
        ],
        compiler_params=params(),
        cost_estimate=cost(2 * slots * store.shape[1] * size * size, 4 * size * size),
        name="gram",
    )(region, table, store, even, odd)

    early = [k for k in steps if not is_late(k, patches)]
    late = [k for k in steps if is_late(k, patches)]
    matrix = jax.ShapeDtypeStruct((size, values), jnp.bfloat16)
    acc, members = pl.pallas_call(
        functools.partial(early_kernel, early),
        out_shape=[jax.ShapeDtypeStruct((size, values), jnp.float32), matrix],
        in_specs=[smem] + [vmem()] * (1 + len(early)),
        out_specs=[vmem()] * 2,
        compiler_params=params(),
        cost_estimate=cost(2 * size * size * values, 2 * size * size + 8 * size * values),
        name="early",
    )(me, gram, *[arrived[k] for k in early])
    back = partners(patches) + [0]
    moved = pl.pallas_call(
        functools.partial(late_kernel, late, back),
        out_shape=[piece_shape] * patches,
        in_specs=[smem] + [vmem()] * (3 + len(late)),
        out_specs=[vmem()] * patches,
        scratch_shapes=[
            pltpu.VMEM((size, values), jnp.bfloat16),
            pltpu.VMEM((size // PARTS, values), jnp.bfloat16),
            pltpu.VMEM((size // 4, values), jnp.float32),
        ],
        compiler_params=params(),
        cost_estimate=cost(3 * size * size * values, 2 * size * size + 10 * size * values),
        name="late",
    )(me, gram, acc, members, *[arrived[k] for k in late])
    order = back
    returned = [ppermute(piece, "member", k) for k, piece in zip(back, moved)]

    steps = rows // rows_per_group(rows, patches)
    fresh = pl.pallas_call(
        functools.partial(merge_kernel, order),
        out_shape=jax.ShapeDtypeStruct((rows * patches, values), jnp.bfloat16),
        in_specs=[smem] + [vmem()] * patches,
        out_specs=pl.BlockSpec(memory_space=pl.ANY),
        scratch_shapes=[
            pltpu.VMEM((rows * patches, values), jnp.bfloat16),
            pltpu.SemaphoreType.DMA((steps,)),
        ],
        compiler_params=params(),
        cost_estimate=cost(2 * 256 * rows * patches * values, 4 * rows * patches * values),
        name="merge",
    )(me, *returned)
    return fresh.reshape(ensemble.shape)


def solution(mesh):
    return jax.shard_map(
        shards,
        mesh=mesh,
        in_specs=(
            P("member", "region", None, None),
            P("region", "member", None, None, None),
            P("region", "member", None),
            P("region", "member", None),
            P("region", "member"),
        ),
        out_specs=P("member", "region", None, None),
        check_vma=False,
    )
```

```python
import functools

import jax
import jax.numpy as jnp
from jax import lax
from jax.experimental import pallas as pl
from jax.experimental.pallas import tpu as pltpu
from jax.sharding import PartitionSpec as P

LIMIT = 16 * 1024 * 1024


def rows_per_group(rows, patches):
    return min(rows, max(16, 256 // patches))


PARTS = 4
WEIGHT = 40


def is_late(k, count):
    return k // (count // PARTS) == PARTS // 2


def partners(count):
    far = list(range(count - 1, count // 2 - 1, -1))
    near = list(range(count // 2 - 1, 0, -1))
    order = []
    for i in range(len(far)):
        order += far[i : i + 1] + near[i : i + 1]
    return order


def inward(count):
    quarter = count // PARTS
    return (
        list(range(count - 1, 3 * quarter - 1, -1))
        + list(range(2 * quarter - 1, 0, -1))
        + list(range(3 * quarter - 1, 2 * quarter - 1, -1))
    )


def ppermute(value, axis, step):
    if step == 0:
        return value
    count = lax.axis_size(axis)
    return lax.ppermute(value, axis, [(i, i ^ step) for i in range(count)])


def split_kernel(steps, me_ref, members_ref, *out_refs):
    patches = len(steps)
    rows = out_refs[0].shape[0]
    group = rows_per_group(rows, patches)
    height = group * patches
    row = lax.broadcasted_iota(jnp.int32, (height, height), 0)
    column = lax.broadcasted_iota(jnp.int32, (height, height), 1)
    source = lax.rem(row, group) * patches + (lax.div(row, group) ^ me_ref[0])
    shuffle = jnp.where(column == source, 1.0, 0.0).astype(jnp.bfloat16)
    for step in range(rows // group):
        block = members_ref[step * height : (step + 1) * height, :]
        moved = jnp.dot(shuffle, block, preferred_element_type=jnp.float32)
        moved = moved.astype(jnp.bfloat16)
        for k, out_ref in zip(steps, out_refs):
            out_ref[step * group : (step + 1) * group, :] = moved[k * group : (k + 1) * group, :]


def merge_kernel(order, me_ref, *refs):
    patches = len(order)
    piece_refs, (out_ref, whole, sem) = dict(zip(order, refs)), refs[patches:]
    rows = piece_refs[0].shape[0]
    group = rows_per_group(rows, patches)
    height = group * patches
    row = lax.broadcasted_iota(jnp.int32, (height, height), 0)
    column = lax.broadcasted_iota(jnp.int32, (height, height), 1)
    source = (lax.rem(row, patches) ^ me_ref[0]) * group + lax.div(row, patches)
    shuffle = jnp.where(column == source, 1.0, 0.0).astype(jnp.bfloat16)
    copies = []
    for step in range(rows // group):
        here = slice(step * group, (step + 1) * group)
        block = jnp.concatenate([piece_refs[k][here, :] for k in range(patches)], axis=0)
        moved = jnp.dot(shuffle, block, preferred_element_type=jnp.float32)
        there = pl.ds(step * height, height)
        whole[there, :] = moved.astype(jnp.bfloat16)
        copies.append(pltpu.make_async_copy(whole.at[there, :], out_ref.at[there, :], sem.at[step]))
        copies[-1].start()
    for copy in copies:
        copy.wait()


def gram_kernel(scale, region_ref, table_ref, own, even, odd, gram_ref, stacked, sem):
    slots = (table_ref.shape[0] - 1) // 2
    rows = own.shape[1]
    parity = lax.rem(region_ref[0], 2)
    count = table_ref[2 * slots]
    for slot in range(slots):
        live = slot < count
        target = stacked.at[pl.ds(slot * rows, rows), :]
        index, source = table_ref[slot], table_ref[slots + slot]
        where = jnp.where(source == 1, 0, jnp.where((source == 2) == (parity == 0), 1, 2))
        for code, store in enumerate((own, even, odd)):

            @pl.when(live & (where == code))
            def _():
                pltpu.make_async_copy(store.at[index], target, sem.at[slot]).start()

        @pl.when(jnp.logical_not(live))
        def _():
            target[...] = jnp.zeros(target.shape, target.dtype)

    for slot in range(slots):

        @pl.when(slot < count)
        def _():
            target = stacked.at[pl.ds(slot * rows, rows), :]
            pltpu.make_async_copy(odd.at[0], target, sem.at[slot]).wait()

    size = gram_ref.shape[0]
    part = min(size, 256)
    for step in range(size // part):
        block = lax.dot_general(
            stacked[:, step * part : (step + 1) * part],
            stacked[...],
            (((0,), (0,)), ((), ())),
            preferred_element_type=jnp.float32,
        )
        gram_ref[step * part : (step + 1) * part, :] = (block * scale).astype(jnp.bfloat16)


def block(me_ref, j, width, rows):
    return pl.ds(pl.multiple_of((lax.div(me_ref[0], width) ^ j) * rows, rows), rows)


def within(me_ref, k, quarter, rows):
    return pl.ds(pl.multiple_of(lax.rem(me_ref[0] ^ k, quarter) * rows, rows), rows)


def ahead_kernel(*refs):
    out_ref = refs[-1]
    for i, piece in enumerate(refs[:-1]):
        out_ref[i] = piece[...]


def early_kernel(steps, me_ref, gram_ref, ahead_ref, *refs):
    piece_refs, (acc_ref, members_ref) = refs[:-2], refs[-2:]
    rows = piece_refs[0].shape[0]
    piece_refs = [ahead_ref.at[i] for i in range(ahead_ref.shape[0])] + list(piece_refs)
    size = gram_ref.shape[0]
    there = block(me_ref, PARTS // 2, size // rows // PARTS, size // PARTS)
    members_ref[there, :] = jnp.zeros((size // PARTS, members_ref.shape[1]), members_ref.dtype)
    for k, piece in zip(steps, piece_refs):
        members_ref[pl.ds(pl.multiple_of((me_ref[0] ^ k) * rows, rows), rows), :] = piece[...]
    tall = size // 4
    for step in range(4):
        here = slice(step * tall, (step + 1) * tall)
        acc_ref[here, :] = jnp.dot(
            gram_ref[here, :], members_ref[...], preferred_element_type=jnp.float32
        )


def late_kernel(late_steps, out_steps, me_ref, *refs):
    count = len(late_steps)
    late_refs, outs = refs[:count], dict(zip(out_steps, refs[count + 3 : -3]))
    gram_ref, acc_ref, members_ref = refs[count : count + 3]
    first, late, fresh = refs[-3:]
    rows = late_refs[0].shape[0]
    size = gram_ref.shape[0]
    width = late.shape[0] // rows
    for k, piece in zip(late_steps, late_refs):
        late[within(me_ref, k, width, rows), :] = piece[...]
    there = block(me_ref, PARTS // 2, width, late.shape[0])
    tall = size // 4
    for step in range(4):
        here = slice(step * tall, (step + 1) * tall)
        part = jnp.dot(gram_ref[here, there], late[...], preferred_element_type=jnp.float32)
        first[here, :] = (acc_ref[here, :] + part).astype(jnp.bfloat16)
    quarter = tall // rows
    for j in (3, 2, 1, 0):
        there = block(me_ref, j, quarter, tall)
        second = jnp.dot(gram_ref[there, :], first[...], preferred_element_type=jnp.float32)
        rest = members_ref[there, :].astype(jnp.float32) - first[there, :].astype(jnp.float32)
        fresh[...] = rest + second
        for k in late_steps:
            if k // quarter == j:
                here = within(me_ref, k, quarter, rows)
                fresh[here, :] += late[within(me_ref, k, width, rows), :].astype(jnp.float32)
        for k, out_ref in outs.items():
            if k // quarter == j:
                here = within(me_ref, k, quarter, rows)
                out_ref[...] = fresh[here, :].astype(jnp.bfloat16)


def vmem():
    return pl.BlockSpec(memory_space=pltpu.VMEM)


def params():
    return pltpu.CompilerParams(vmem_limit_bytes=LIMIT)


def cost(flops, nbytes):
    return pl.CostEstimate(flops=flops, bytes_accessed=nbytes, transcendentals=0)


def swap(store, first):
    count = lax.axis_size("region")
    pairs = [(i, i + 1) for i in range(first, count - 1, 2)]
    return lax.ppermute(store, "region", pairs + [(j, i) for i, j in pairs])


def shards(ensemble, obs_store, block_ids, block_src, block_count):
    rows, _, patches, values = ensemble.shape
    store = obs_store.reshape(obs_store.shape[2:])
    size = store.shape[2]
    slots = block_ids.shape[2]
    me = lax.axis_index("member").astype(jnp.int32).reshape(1)
    region = lax.axis_index("region").astype(jnp.int32).reshape(1)
    smem = pl.BlockSpec(memory_space=pltpu.SMEM)
    hbm = pl.BlockSpec(memory_space=pltpu.HBM)
    piece_shape = jax.ShapeDtypeStruct((rows, values), jnp.bfloat16)

    steps = [0] + inward(patches)
    pieces = pl.pallas_call(
        functools.partial(split_kernel, steps),
        out_shape=[piece_shape] * patches,
        in_specs=[smem, vmem()],
        out_specs=[vmem()] * patches,
        compiler_params=params(),
        cost_estimate=cost(2 * 256 * rows * patches * values, 4 * rows * patches * values),
        name="split",
    )(me, ensemble.reshape(rows * patches, values))
    arrived = {k: ppermute(piece, "member", k) for k, piece in zip(steps, pieces)}
    store, _ = lax.optimization_barrier((store, pieces[0]))
    odd, even = swap(store, 1), swap(store, 0)

    table = jnp.concatenate([block_ids.ravel(), block_src.ravel(), block_count.ravel()])
    gram = pl.pallas_call(
        functools.partial(gram_kernel, 1.0 / (2.0 * size)),
        out_shape=jax.ShapeDtypeStruct((size, size), jnp.bfloat16),
        in_specs=[smem] * 2 + [hbm] * 3,
        out_specs=vmem(),
        scratch_shapes=[
            pltpu.VMEM((slots * store.shape[1], size), jnp.bfloat16),
            pltpu.SemaphoreType.DMA((slots,)),
        ],
        compiler_params=params(),
        cost_estimate=cost(2 * slots * store.shape[1] * size * size, 4 * size * size),
        name="gram",
    )(region, table, store, even, odd)

    early = [k for k in steps if k and not is_late(k, patches)]
    late = [k for k in steps if is_late(k, patches)]
    matrix = jax.ShapeDtypeStruct((size, values), jnp.bfloat16)
    count = patches // PARTS + 1
    first_steps, early = early[:count], early[count:] + [0]
    ahead = pl.pallas_call(
        ahead_kernel,
        out_shape=jax.ShapeDtypeStruct((count, rows, values), jnp.bfloat16),
        in_specs=[vmem()] * count,
        out_specs=vmem(),
        compiler_params=params(),
        cost_estimate=cost(WEIGHT * size * size * values, 4 * count * rows * values),
        name="ahead",
    )(*[arrived[k] for k in first_steps])
    acc, members = pl.pallas_call(
        functools.partial(early_kernel, first_steps + early),
        out_shape=[jax.ShapeDtypeStruct((size, values), jnp.float32), matrix],
        in_specs=[smem] + [vmem()] * (2 + len(early)),
        out_specs=[vmem()] * 2,
        compiler_params=params(),
        cost_estimate=cost(1, 1),
        name="early",
    )(me, gram, ahead, *[arrived[k] for k in early])
    back = partners(patches) + [0]
    moved = pl.pallas_call(
        functools.partial(late_kernel, late, back),
        out_shape=[piece_shape] * patches,
        in_specs=[smem] + [vmem()] * (3 + len(late)),
        out_specs=[vmem()] * patches,
        scratch_shapes=[
            pltpu.VMEM((size, values), jnp.bfloat16),
            pltpu.VMEM((size // PARTS, values), jnp.bfloat16),
            pltpu.VMEM((size // 4, values), jnp.float32),
        ],
        compiler_params=params(),
        cost_estimate=cost(3 * size * size * values, 2 * size * size + 10 * size * values),
        name="late",
    )(me, *[arrived[k] for k in late], gram, acc, members)
    order = back
    returned = [ppermute(piece, "member", k) for k, piece in zip(back, moved)]

    steps = rows // rows_per_group(rows, patches)
    fresh = pl.pallas_call(
        functools.partial(merge_kernel, order),
        out_shape=jax.ShapeDtypeStruct((rows * patches, values), jnp.bfloat16),
        in_specs=[smem] + [vmem()] * patches,
        out_specs=pl.BlockSpec(memory_space=pl.ANY),
        scratch_shapes=[
            pltpu.VMEM((rows * patches, values), jnp.bfloat16),
            pltpu.SemaphoreType.DMA((steps,)),
        ],
        compiler_params=params(),
        cost_estimate=cost(2 * 256 * rows * patches * values, 4 * rows * patches * values),
        name="merge",
    )(me, *returned)
    return fresh.reshape(ensemble.shape)


def solution(mesh):
    return jax.shard_map(
        shards,
        mesh=mesh,
        in_specs=(
            P("member", "region", None, None),
            P("region", "member", None, None, None),
            P("region", "member", None),
            P("region", "member", None),
            P("region", "member"),
        ),
        out_specs=P("member", "region", None, None),
        check_vma=False,
    )
```

```python
import functools

import jax
import jax.numpy as jnp
from jax import lax
from jax.experimental import pallas as pl
from jax.experimental.pallas import tpu as pltpu
from jax.sharding import PartitionSpec as P

LIMIT = 16 * 1024 * 1024


def rows_per_group(rows, patches):
    return min(rows, max(16, 256 // patches))


PARTS = 4
WEIGHT = 40


def is_late(k, count):
    return k // (count // PARTS) == PARTS // 2


def partners(count):
    far = list(range(count - 1, count // 2 - 1, -1))
    near = list(range(count // 2 - 1, 0, -1))
    order = []
    for i in range(len(far)):
        order += far[i : i + 1] + near[i : i + 1]
    return order


def inward(count):
    quarter = count // PARTS
    near = list(range(2 * quarter - 1, 0, -1))
    far = list(range(count - 1, 3 * quarter - 1, -1))
    return near[:1] + far + near[1:] + list(range(3 * quarter - 1, 2 * quarter - 1, -1))


def ppermute(value, axis, step):
    if step == 0:
        return value
    count = lax.axis_size(axis)
    return lax.ppermute(value, axis, [(i, i ^ step) for i in range(count)])


def split_kernel(steps, me_ref, members_ref, *out_refs):
    patches = len(steps)
    rows = out_refs[0].shape[0]
    group = rows_per_group(rows, patches)
    height = group * patches
    row = lax.broadcasted_iota(jnp.int32, (height, height), 0)
    column = lax.broadcasted_iota(jnp.int32, (height, height), 1)
    source = lax.rem(row, group) * patches + (lax.div(row, group) ^ me_ref[0])
    shuffle = jnp.where(column == source, 1.0, 0.0).astype(jnp.bfloat16)
    for step in range(rows // group):
        block = members_ref[step * height : (step + 1) * height, :]
        moved = jnp.dot(shuffle, block, preferred_element_type=jnp.float32)
        moved = moved.astype(jnp.bfloat16)
        for k, out_ref in zip(steps, out_refs):
            out_ref[step * group : (step + 1) * group, :] = moved[k * group : (k + 1) * group, :]


def merge_kernel(order, me_ref, *refs):
    patches = len(order)
    piece_refs, (out_ref, whole, sem) = dict(zip(order, refs)), refs[patches:]
    rows = piece_refs[0].shape[0]
    group = rows_per_group(rows, patches)
    height = group * patches
    row = lax.broadcasted_iota(jnp.int32, (height, height), 0)
    column = lax.broadcasted_iota(jnp.int32, (height, height), 1)
    source = (lax.rem(row, patches) ^ me_ref[0]) * group + lax.div(row, patches)
    shuffle = jnp.where(column == source, 1.0, 0.0).astype(jnp.bfloat16)
    copies = []
    for step in range(rows // group):
        here = slice(step * group, (step + 1) * group)
        block = jnp.concatenate([piece_refs[k][here, :] for k in range(patches)], axis=0)
        moved = jnp.dot(shuffle, block, preferred_element_type=jnp.float32)
        there = pl.ds(step * height, height)
        whole[there, :] = moved.astype(jnp.bfloat16)
        copies.append(pltpu.make_async_copy(whole.at[there, :], out_ref.at[there, :], sem.at[step]))
        copies[-1].start()
    for copy in copies:
        copy.wait()


def gram_kernel(scale, region_ref, table_ref, own, even, odd, gram_ref, stacked, sem):
    slots = (table_ref.shape[0] - 1) // 2
    rows = own.shape[1]
    parity = lax.rem(region_ref[0], 2)
    count = table_ref[2 * slots]
    for slot in range(slots):
        live = slot < count
        target = stacked.at[pl.ds(slot * rows, rows), :]
        index, source = table_ref[slot], table_ref[slots + slot]
        where = jnp.where(source == 1, 0, jnp.where((source == 2) == (parity == 0), 1, 2))
        for code, store in enumerate((own, even, odd)):

            @pl.when(live & (where == code))
            def _():
                pltpu.make_async_copy(store.at[index], target, sem.at[slot]).start()

        @pl.when(jnp.logical_not(live))
        def _():
            target[...] = jnp.zeros(target.shape, target.dtype)

    for slot in range(slots):

        @pl.when(slot < count)
        def _():
            target = stacked.at[pl.ds(slot * rows, rows), :]
            pltpu.make_async_copy(odd.at[0], target, sem.at[slot]).wait()

    size = gram_ref.shape[0]
    part = min(size, 256)
    for step in range(size // part):
        block = lax.dot_general(
            stacked[:, step * part : (step + 1) * part],
            stacked[...],
            (((0,), (0,)), ((), ())),
            preferred_element_type=jnp.float32,
        )
        gram_ref[step * part : (step + 1) * part, :] = (block * scale).astype(jnp.bfloat16)


def block(me_ref, j, width, rows):
    return pl.ds(pl.multiple_of((lax.div(me_ref[0], width) ^ j) * rows, rows), rows)


def within(me_ref, k, quarter, rows):
    return pl.ds(pl.multiple_of(lax.rem(me_ref[0] ^ k, quarter) * rows, rows), rows)


def ahead_kernel(*refs):
    out_ref = refs[-1]
    for i, piece in enumerate(refs[:-1]):
        out_ref[i] = piece[...]


def early_kernel(steps, me_ref, gram_ref, ahead_ref, *refs):
    piece_refs, (acc_ref, members_ref) = refs[:-2], refs[-2:]
    rows = piece_refs[0].shape[0]
    piece_refs = [ahead_ref.at[i] for i in range(ahead_ref.shape[0])] + list(piece_refs)
    size = gram_ref.shape[0]
    there = block(me_ref, PARTS // 2, size // rows // PARTS, size // PARTS)
    members_ref[there, :] = jnp.zeros((size // PARTS, members_ref.shape[1]), members_ref.dtype)
    for k, piece in zip(steps, piece_refs):
        members_ref[pl.ds(pl.multiple_of((me_ref[0] ^ k) * rows, rows), rows), :] = piece[...]
    tall = size // 4
    for step in range(4):
        here = slice(step * tall, (step + 1) * tall)
        acc_ref[here, :] = jnp.dot(
            gram_ref[here, :], members_ref[...], preferred_element_type=jnp.float32
        )


def late_kernel(late_steps, out_steps, me_ref, *refs):
    count = len(late_steps)
    late_refs, outs = refs[:count], dict(zip(out_steps, refs[count + 3 : -3]))
    gram_ref, acc_ref, members_ref = refs[count : count + 3]
    first, late, fresh = refs[-3:]
    rows = late_refs[0].shape[0]
    size = gram_ref.shape[0]
    width = late.shape[0] // rows
    for k, piece in zip(late_steps, late_refs):
        late[within(me_ref, k, width, rows), :] = piece[...]
    there = block(me_ref, PARTS // 2, width, late.shape[0])
    tall = size // 4
    for step in range(4):
        here = slice(step * tall, (step + 1) * tall)
        part = jnp.dot(gram_ref[here, there], late[...], preferred_element_type=jnp.float32)
        first[here, :] = (acc_ref[here, :] + part).astype(jnp.bfloat16)
    quarter = tall // rows
    for j in (3, 2, 1, 0):
        there = block(me_ref, j, quarter, tall)
        second = jnp.dot(gram_ref[there, :], first[...], preferred_element_type=jnp.float32)
        rest = members_ref[there, :].astype(jnp.float32) - first[there, :].astype(jnp.float32)
        fresh[...] = rest + second
        for k in late_steps:
            if k // quarter == j:
                here = within(me_ref, k, quarter, rows)
                fresh[here, :] += late[within(me_ref, k, width, rows), :].astype(jnp.float32)
        for k, out_ref in outs.items():
            if k // quarter == j:
                here = within(me_ref, k, quarter, rows)
                out_ref[...] = fresh[here, :].astype(jnp.bfloat16)


def vmem():
    return pl.BlockSpec(memory_space=pltpu.VMEM)


def params():
    return pltpu.CompilerParams(vmem_limit_bytes=LIMIT)


def cost(flops, nbytes):
    return pl.CostEstimate(flops=flops, bytes_accessed=nbytes, transcendentals=0)


def swap(store, first):
    count = lax.axis_size("region")
    pairs = [(i, i + 1) for i in range(first, count - 1, 2)]
    return lax.ppermute(store, "region", pairs + [(j, i) for i, j in pairs])


def shards(ensemble, obs_store, block_ids, block_src, block_count):
    rows, _, patches, values = ensemble.shape
    store = obs_store.reshape(obs_store.shape[2:])
    size = store.shape[2]
    slots = block_ids.shape[2]
    me = lax.axis_index("member").astype(jnp.int32).reshape(1)
    region = lax.axis_index("region").astype(jnp.int32).reshape(1)
    smem = pl.BlockSpec(memory_space=pltpu.SMEM)
    anywhere = pl.BlockSpec(memory_space=pl.ANY)
    piece_shape = jax.ShapeDtypeStruct((rows, values), jnp.bfloat16)

    steps = [0] + inward(patches)
    pieces = pl.pallas_call(
        functools.partial(split_kernel, steps),
        out_shape=[piece_shape] * patches,
        in_specs=[smem, vmem()],
        out_specs=[vmem()] * patches,
        compiler_params=params(),
        cost_estimate=cost(2 * 256 * rows * patches * values, 4 * rows * patches * values),
        name="split",
    )(me, ensemble.reshape(rows * patches, values))
    arrived = {k: ppermute(piece, "member", k) for k, piece in zip(steps, pieces)}
    store, _ = lax.optimization_barrier((store, pieces[0]))
    odd, even = swap(store, 1), swap(store, 0)

    table = jnp.concatenate([block_ids.ravel(), block_src.ravel(), block_count.ravel()])
    gram = pl.pallas_call(
        functools.partial(gram_kernel, 1.0 / (2.0 * size)),
        out_shape=jax.ShapeDtypeStruct((size, size), jnp.bfloat16),
        in_specs=[smem] * 2 + [anywhere] * 3,
        out_specs=vmem(),
        scratch_shapes=[
            pltpu.VMEM((slots * store.shape[1], size), jnp.bfloat16),
            pltpu.SemaphoreType.DMA((slots,)),
        ],
        compiler_params=params(),
        cost_estimate=cost(2 * slots * store.shape[1] * size * size, 4 * size * size),
        name="gram",
    )(region, table, store, even, odd)

    early = [k for k in steps if k and not is_late(k, patches)]
    late = [k for k in steps if is_late(k, patches)]
    matrix = jax.ShapeDtypeStruct((size, values), jnp.bfloat16)
    count = patches // PARTS + 1
    first_steps, early = early[:count], early[count:] + [0]
    ahead = pl.pallas_call(
        ahead_kernel,
        out_shape=jax.ShapeDtypeStruct((count, rows, values), jnp.bfloat16),
        in_specs=[vmem()] * count,
        out_specs=vmem(),
        compiler_params=params(),
        cost_estimate=cost(WEIGHT * size * size * values, 4 * count * rows * values),
        name="ahead",
    )(*[arrived[k] for k in first_steps])
    acc, members = pl.pallas_call(
        functools.partial(early_kernel, first_steps + early),
        out_shape=[jax.ShapeDtypeStruct((size, values), jnp.float32), matrix],
        in_specs=[smem] + [vmem()] * (2 + len(early)),
        out_specs=[vmem()] * 2,
        compiler_params=params(),
        cost_estimate=cost(1, 1),
        name="early",
    )(me, gram, ahead, *[arrived[k] for k in early])
    back = partners(patches) + [0]
    moved = pl.pallas_call(
        functools.partial(late_kernel, late, back),
        out_shape=[piece_shape] * patches,
        in_specs=[smem] + [vmem()] * (3 + len(late)),
        out_specs=[vmem()] * patches,
        scratch_shapes=[
            pltpu.VMEM((size, values), jnp.bfloat16),
            pltpu.VMEM((size // PARTS, values), jnp.bfloat16),
            pltpu.VMEM((size // 4, values), jnp.float32),
        ],
        compiler_params=params(),
        cost_estimate=cost(3 * size * size * values, 2 * size * size + 10 * size * values),
        name="late",
    )(me, *[arrived[k] for k in late], gram, acc, members)
    order = back
    returned = [ppermute(piece, "member", k) for k, piece in zip(back, moved)]

    steps = rows // rows_per_group(rows, patches)
    fresh = pl.pallas_call(
        functools.partial(merge_kernel, order),
        out_shape=jax.ShapeDtypeStruct((rows * patches, values), jnp.bfloat16),
        in_specs=[smem] + [vmem()] * patches,
        out_specs=pl.BlockSpec(memory_space=pl.ANY),
        scratch_shapes=[
            pltpu.VMEM((rows * patches, values), jnp.bfloat16),
            pltpu.SemaphoreType.DMA((steps,)),
        ],
        compiler_params=params(),
        cost_estimate=cost(2 * 256 * rows * patches * values, 4 * rows * patches * values),
        name="merge",
    )(me, *returned)
    return fresh.reshape(ensemble.shape)


def solution(mesh):
    return jax.shard_map(
        shards,
        mesh=mesh,
        in_specs=(
            P("member", "region", None, None),
            P("region", "member", None, None, None),
            P("region", "member", None),
            P("region", "member", None),
            P("region", "member"),
        ),
        out_specs=P("member", "region", None, None),
        check_vma=False,
    )
```

```python
import functools

import jax
import jax.numpy as jnp
from jax import lax
from jax.experimental import pallas as pl
from jax.experimental.pallas import tpu as pltpu
from jax.sharding import PartitionSpec as P

LIMIT = 16 * 1024 * 1024


def rows_per_group(rows, patches):
    return min(rows, max(16, 256 // patches))


PARTS = 4
WEIGHT = 40


def is_late(k, count):
    return k // (count // PARTS) == PARTS // 2


def partners(count):
    far = list(range(count - 1, count // 2 - 1, -1))
    near = list(range(count // 2 - 1, 0, -1))
    order = []
    for i in range(len(far)):
        order += far[i : i + 1] + near[i : i + 1]
    return order


def inward(count):
    quarter = count // PARTS
    return (
        list(range(count - 1, 3 * quarter - 1, -1))
        + list(range(2 * quarter - 1, 0, -1))
        + list(range(3 * quarter - 1, 2 * quarter - 1, -1))
    )


def ppermute(value, axis, step):
    if step == 0:
        return value
    count = lax.axis_size(axis)
    return lax.ppermute(value, axis, [(i, i ^ step) for i in range(count)])


def split_kernel(steps, me_ref, members_ref, *out_refs):
    patches = len(steps)
    rows = out_refs[0].shape[0]
    group = rows_per_group(rows, patches)
    height = group * patches
    row = lax.broadcasted_iota(jnp.int32, (height, height), 0)
    column = lax.broadcasted_iota(jnp.int32, (height, height), 1)
    source = lax.rem(row, group) * patches + (lax.div(row, group) ^ me_ref[0])
    shuffle = jnp.where(column == source, 1.0, 0.0).astype(jnp.bfloat16)
    for step in range(rows // group):
        block = members_ref[step * height : (step + 1) * height, :]
        moved = jnp.dot(shuffle, block, preferred_element_type=jnp.float32)
        moved = moved.astype(jnp.bfloat16)
        for k, out_ref in zip(steps, out_refs):
            out_ref[step * group : (step + 1) * group, :] = moved[k * group : (k + 1) * group, :]


def merge_kernel(order, me_ref, *refs):
    patches = len(order)
    piece_refs, (out_ref, whole, sem) = dict(zip(order, refs)), refs[patches:]
    rows = piece_refs[0].shape[0]
    group = rows_per_group(rows, patches)
    height = group * patches
    row = lax.broadcasted_iota(jnp.int32, (height, height), 0)
    column = lax.broadcasted_iota(jnp.int32, (height, height), 1)
    source = (lax.rem(row, patches) ^ me_ref[0]) * group + lax.div(row, patches)
    shuffle = jnp.where(column == source, 1.0, 0.0).astype(jnp.bfloat16)
    copies = []
    for step in range(rows // group):
        here = slice(step * group, (step + 1) * group)
        block = jnp.concatenate([piece_refs[k][here, :] for k in range(patches)], axis=0)
        moved = jnp.dot(shuffle, block, preferred_element_type=jnp.float32)
        there = pl.ds(step * height, height)
        whole[there, :] = moved.astype(jnp.bfloat16)
        copies.append(pltpu.make_async_copy(whole.at[there, :], out_ref.at[there, :], sem.at[step]))
        copies[-1].start()
    for copy in copies:
        copy.wait()


def gram_kernel(scale, region_ref, table_ref, own, odd, even, gram_ref, stacked, sem):
    slots = (table_ref.shape[0] - 1) // 2
    rows = own.shape[1]
    parity = lax.rem(region_ref[0], 2)
    count = table_ref[2 * slots]
    for slot in range(slots):
        live = slot < count
        target = stacked.at[pl.ds(slot * rows, rows), :]
        index, source = table_ref[slot], table_ref[slots + slot]
        where = jnp.where(source == 1, 0, jnp.where((source == 2) == (parity == 0), 1, 2))
        for code, store in enumerate((own, even, odd)):

            @pl.when(live & (where == code))
            def _():
                pltpu.make_async_copy(store.at[index], target, sem.at[slot]).start()

        @pl.when(jnp.logical_not(live))
        def _():
            target[...] = jnp.zeros(target.shape, target.dtype)

    for slot in range(slots):

        @pl.when(slot < count)
        def _():
            target = stacked.at[pl.ds(slot * rows, rows), :]
            pltpu.make_async_copy(odd.at[0], target, sem.at[slot]).wait()

    size = gram_ref.shape[0]
    part = min(size, 256)
    for step in range(size // part):
        block = lax.dot_general(
            stacked[:, step * part : (step + 1) * part],
            stacked[...],
            (((0,), (0,)), ((), ())),
            preferred_element_type=jnp.float32,
        )
        gram_ref[step * part : (step + 1) * part, :] = (block * scale).astype(jnp.bfloat16)


def ahead_kernel(*refs):
    token = refs[-1]
    token[...] = jnp.zeros(token.shape, token.dtype)


def transform_kernel(steps, out_steps, me_ref, *refs):
    count = len(steps)
    pieces, outs = dict(zip(steps, refs)), dict(zip(out_steps, refs[count + 2 : -3]))
    gram_ref = refs[count]
    members, first, fresh = refs[-3:]
    rows = pieces[0].shape[0]

    def place(k):
        return pl.ds(pl.multiple_of((me_ref[0] ^ k) * rows, rows), rows)

    for k, piece in pieces.items():
        members[place(k), :] = piece[...]
    size = gram_ref.shape[0]
    part = min(size, 256)
    for step in range(size // part):
        here = slice(step * part, (step + 1) * part)
        first[here, :] = jnp.dot(
            gram_ref[here, :], members[...], preferred_element_type=jnp.float32
        ).astype(jnp.bfloat16)
    for step in range(size // part):
        here = slice(step * part, (step + 1) * part)
        second = jnp.dot(gram_ref[here, :], first[...], preferred_element_type=jnp.float32)
        rest = members[here, :].astype(jnp.float32) - first[here, :].astype(jnp.float32)
        fresh[here, :] = (rest + second).astype(jnp.bfloat16)
    for k, out_ref in outs.items():
        out_ref[...] = fresh[place(k), :]


def vmem():
    return pl.BlockSpec(memory_space=pltpu.VMEM)


def params():
    return pltpu.CompilerParams(vmem_limit_bytes=LIMIT)


def cost(flops, nbytes):
    return pl.CostEstimate(flops=flops, bytes_accessed=nbytes, transcendentals=0)


def swap(store, first):
    count = lax.axis_size("region")
    pairs = [(i, i + 1) for i in range(first, count - 1, 2)]
    return lax.ppermute(store, "region", pairs + [(j, i) for i, j in pairs])


def shards(ensemble, obs_store, block_ids, block_src, block_count):
    rows, _, patches, values = ensemble.shape
    store = obs_store.reshape(obs_store.shape[2:])
    size = store.shape[2]
    slots = block_ids.shape[2]
    me = lax.axis_index("member").astype(jnp.int32).reshape(1)
    region = lax.axis_index("region").astype(jnp.int32).reshape(1)
    smem = pl.BlockSpec(memory_space=pltpu.SMEM)
    anywhere = pl.BlockSpec(memory_space=pl.ANY)
    piece_shape = jax.ShapeDtypeStruct((rows, values), jnp.bfloat16)

    steps = [0] + inward(patches)
    pieces = pl.pallas_call(
        functools.partial(split_kernel, steps),
        out_shape=[piece_shape] * patches,
        in_specs=[smem, vmem()],
        out_specs=[vmem()] * patches,
        compiler_params=params(),
        cost_estimate=cost(2 * 256 * rows * patches * values, 4 * rows * patches * values),
        name="split",
    )(me, ensemble.reshape(rows * patches, values))
    arrived = {k: ppermute(piece, "member", k) for k, piece in zip(steps, pieces)}
    store, _ = lax.optimization_barrier((store, pieces[0]))
    odd, even = swap(store, 1), swap(store, 0)

    table = jnp.concatenate([block_ids.ravel(), block_src.ravel(), block_count.ravel()])
    gram = pl.pallas_call(
        functools.partial(gram_kernel, 1.0 / (2.0 * size)),
        out_shape=jax.ShapeDtypeStruct((size, size), jnp.bfloat16),
        in_specs=[smem] * 2 + [anywhere] * 3,
        out_specs=vmem(),
        scratch_shapes=[
            pltpu.VMEM((slots * store.shape[1], size), jnp.bfloat16),
            pltpu.SemaphoreType.DMA((slots,)),
        ],
        compiler_params=params(),
        cost_estimate=cost(2 * slots * store.shape[1] * size * size, 4 * size * size),
        name="gram",
    )(region, table, store, odd, even)

    count = patches // PARTS + 1
    first_steps = steps[1 : count + 1]
    token = pl.pallas_call(
        ahead_kernel,
        out_shape=jax.ShapeDtypeStruct((8, 128), jnp.float32),
        in_specs=[anywhere] * count,
        out_specs=vmem(),
        compiler_params=params(),
        cost_estimate=cost(WEIGHT * size * size * values, 4 * count * rows * values),
        name="ahead",
    )(*[arrived[k] for k in first_steps])
    late = [k for k in steps if is_late(k, patches)]
    middle = [k for k in steps[count + 1 :] if k not in late]
    steps = late + middle + first_steps + [0]
    back = partners(patches) + [0]
    moved = pl.pallas_call(
        functools.partial(transform_kernel, steps, back),
        out_shape=[piece_shape] * patches,
        in_specs=[smem] + [vmem()] * (patches + 1) + [anywhere],
        out_specs=[vmem()] * patches,
        scratch_shapes=[pltpu.VMEM((size, values), jnp.bfloat16)] * 3,
        compiler_params=params(),
        cost_estimate=cost(4 * size * size * values, 2 * size * size + 4 * size * values),
        name="transform",
    )(me, *[arrived[k] for k in steps], gram, token)
    order = back
    returned = [ppermute(piece, "member", k) for k, piece in zip(back, moved)]

    steps = rows // rows_per_group(rows, patches)
    fresh = pl.pallas_call(
        functools.partial(merge_kernel, order),
        out_shape=jax.ShapeDtypeStruct((rows * patches, values), jnp.bfloat16),
        in_specs=[smem] + [vmem()] * patches,
        out_specs=pl.BlockSpec(memory_space=pl.ANY),
        scratch_shapes=[
            pltpu.VMEM((rows * patches, values), jnp.bfloat16),
            pltpu.SemaphoreType.DMA((steps,)),
        ],
        compiler_params=params(),
        cost_estimate=cost(2 * 256 * rows * patches * values, 4 * rows * patches * values),
        name="merge",
    )(me, *returned)
    return fresh.reshape(ensemble.shape)


def solution(mesh):
    return jax.shard_map(
        shards,
        mesh=mesh,
        in_specs=(
            P("member", "region", None, None),
            P("region", "member", None, None, None),
            P("region", "member", None),
            P("region", "member", None),
            P("region", "member"),
        ),
        out_specs=P("member", "region", None, None),
        check_vma=False,
    )
```

```python
import functools

import jax
import jax.numpy as jnp
from jax import lax
from jax.experimental import pallas as pl
from jax.experimental.pallas import tpu as pltpu
from jax.sharding import PartitionSpec as P

LIMIT = 16 * 1024 * 1024


def rows_per_group(rows, patches):
    return min(rows, max(16, 256 // patches))


PARTS = 4
WEIGHT = 40


def is_late(k, count):
    return k // (count // PARTS) == PARTS // 2


def partners(count):
    far = list(range(count - 1, count // 2 - 1, -1))
    near = list(range(count // 2 - 1, 0, -1))
    order = []
    for i in range(len(far)):
        order += far[i : i + 1] + near[i : i + 1]
    return order


def inward(count):
    quarter = count // PARTS
    return (
        list(range(count - 1, 3 * quarter - 1, -1))
        + list(range(2 * quarter - 1, 0, -1))
        + list(range(3 * quarter - 1, 2 * quarter - 1, -1))
    )


def ppermute(value, axis, step):
    if step == 0:
        return value
    count = lax.axis_size(axis)
    return lax.ppermute(value, axis, [(i, i ^ step) for i in range(count)])


def split_kernel(steps, me_ref, members_ref, *refs):
    out_refs, token = refs[:-1], refs[-1]
    token[...] = jnp.zeros(token.shape, token.dtype)
    patches = len(steps)
    rows = out_refs[0].shape[0]
    group = rows_per_group(rows, patches)
    height = group * patches
    row = lax.broadcasted_iota(jnp.int32, (height, height), 0)
    column = lax.broadcasted_iota(jnp.int32, (height, height), 1)
    source = lax.rem(row, group) * patches + (lax.div(row, group) ^ me_ref[0])
    shuffle = jnp.where(column == source, 1.0, 0.0).astype(jnp.bfloat16)
    for step in range(rows // group):
        block = members_ref[step * height : (step + 1) * height, :]
        moved = jnp.dot(shuffle, block, preferred_element_type=jnp.float32)
        moved = moved.astype(jnp.bfloat16)
        for k, out_ref in zip(steps, out_refs):
            out_ref[step * group : (step + 1) * group, :] = moved[k * group : (k + 1) * group, :]


def merge_kernel(order, me_ref, *refs):
    patches = len(order)
    piece_refs, (out_ref, whole, sem) = dict(zip(order, refs)), refs[patches:]
    rows = piece_refs[0].shape[0]
    group = rows_per_group(rows, patches)
    height = group * patches
    row = lax.broadcasted_iota(jnp.int32, (height, height), 0)
    column = lax.broadcasted_iota(jnp.int32, (height, height), 1)
    source = (lax.rem(row, patches) ^ me_ref[0]) * group + lax.div(row, patches)
    shuffle = jnp.where(column == source, 1.0, 0.0).astype(jnp.bfloat16)
    copies = []
    for step in range(rows // group):
        here = slice(step * group, (step + 1) * group)
        block = jnp.concatenate([piece_refs[k][here, :] for k in range(patches)], axis=0)
        moved = jnp.dot(shuffle, block, preferred_element_type=jnp.float32)
        there = pl.ds(step * height, height)
        whole[there, :] = moved.astype(jnp.bfloat16)
        copies.append(pltpu.make_async_copy(whole.at[there, :], out_ref.at[there, :], sem.at[step]))
        copies[-1].start()
    for copy in copies:
        copy.wait()


def gram_kernel(scale, region_ref, table_ref, own, even, odd, gram_ref, stacked, sem):
    slots = (table_ref.shape[0] - 1) // 2
    rows = own.shape[1]
    parity = lax.rem(region_ref[0], 2)
    count = table_ref[2 * slots]
    for slot in range(slots):
        live = slot < count
        target = stacked.at[pl.ds(slot * rows, rows), :]
        index, source = table_ref[slot], table_ref[slots + slot]
        where = jnp.where(source == 1, 0, jnp.where((source == 2) == (parity == 0), 1, 2))
        for code, store in enumerate((own, even, odd)):

            @pl.when(live & (where == code))
            def _():
                pltpu.make_async_copy(store.at[index], target, sem.at[slot]).start()

        @pl.when(jnp.logical_not(live))
        def _():
            target[...] = jnp.zeros(target.shape, target.dtype)

    for slot in range(slots):

        @pl.when(slot < count)
        def _():
            target = stacked.at[pl.ds(slot * rows, rows), :]
            pltpu.make_async_copy(odd.at[0], target, sem.at[slot]).wait()

    size = gram_ref.shape[0]
    part = min(size, 256)
    for step in range(size // part):
        block = lax.dot_general(
            stacked[:, step * part : (step + 1) * part],
            stacked[...],
            (((0,), (0,)), ((), ())),
            preferred_element_type=jnp.float32,
        )
        gram_ref[step * part : (step + 1) * part, :] = (block * scale).astype(jnp.bfloat16)


def block(me_ref, j, width, rows):
    return pl.ds(pl.multiple_of((lax.div(me_ref[0], width) ^ j) * rows, rows), rows)


def within(me_ref, k, quarter, rows):
    return pl.ds(pl.multiple_of(lax.rem(me_ref[0] ^ k, quarter) * rows, rows), rows)


def ahead_kernel(*refs):
    refs[-1][...] = refs[0][...]


def early_kernel(steps, me_ref, gram_ref, token, *refs):
    piece_refs, (acc_ref, members_ref) = refs[:-2], refs[-2:]
    rows = piece_refs[0].shape[0]
    size = gram_ref.shape[0]
    there = block(me_ref, PARTS // 2, size // rows // PARTS, size // PARTS)
    members_ref[there, :] = jnp.zeros((size // PARTS, members_ref.shape[1]), members_ref.dtype)
    for k, piece in zip(steps, piece_refs):
        members_ref[pl.ds(pl.multiple_of((me_ref[0] ^ k) * rows, rows), rows), :] = piece[...]
    tall = size // 4
    for step in range(4):
        here = slice(step * tall, (step + 1) * tall)
        acc_ref[here, :] = jnp.dot(
            gram_ref[here, :], members_ref[...], preferred_element_type=jnp.float32
        )


def late_kernel(late_steps, out_steps, me_ref, *refs):
    count = len(late_steps)
    late_refs, outs = refs[:count], dict(zip(out_steps, refs[count + 3 : -3]))
    gram_ref, acc_ref, members_ref = refs[count : count + 3]
    first, late, fresh = refs[-3:]
    rows = late_refs[0].shape[0]
    size = gram_ref.shape[0]
    width = late.shape[0] // rows
    for k, piece in zip(late_steps, late_refs):
        late[within(me_ref, k, width, rows), :] = piece[...]
    there = block(me_ref, PARTS // 2, width, late.shape[0])
    tall = size // 4
    for step in range(4):
        here = slice(step * tall, (step + 1) * tall)
        part = jnp.dot(gram_ref[here, there], late[...], preferred_element_type=jnp.float32)
        first[here, :] = (acc_ref[here, :] + part).astype(jnp.bfloat16)
    quarter = tall // rows
    for j in (3, 2, 1, 0):
        there = block(me_ref, j, quarter, tall)
        second = jnp.dot(gram_ref[there, :], first[...], preferred_element_type=jnp.float32)
        rest = members_ref[there, :].astype(jnp.float32) - first[there, :].astype(jnp.float32)
        fresh[...] = rest + second
        for k in late_steps:
            if k // quarter == j:
                here = within(me_ref, k, quarter, rows)
                fresh[here, :] += late[within(me_ref, k, width, rows), :].astype(jnp.float32)
        for k, out_ref in outs.items():
            if k // quarter == j:
                here = within(me_ref, k, quarter, rows)
                out_ref[...] = fresh[here, :].astype(jnp.bfloat16)


def vmem():
    return pl.BlockSpec(memory_space=pltpu.VMEM)


def params():
    return pltpu.CompilerParams(vmem_limit_bytes=LIMIT)


def cost(flops, nbytes):
    return pl.CostEstimate(flops=flops, bytes_accessed=nbytes, transcendentals=0)


def swap(store, first):
    count = lax.axis_size("region")
    pairs = [(i, i + 1) for i in range(first, count - 1, 2)]
    return lax.ppermute(store, "region", pairs + [(j, i) for i, j in pairs])


def shards(ensemble, obs_store, block_ids, block_src, block_count):
    rows, _, patches, values = ensemble.shape
    store = obs_store.reshape(obs_store.shape[2:])
    size = store.shape[2]
    slots = block_ids.shape[2]
    me = lax.axis_index("member").astype(jnp.int32).reshape(1)
    region = lax.axis_index("region").astype(jnp.int32).reshape(1)
    smem = pl.BlockSpec(memory_space=pltpu.SMEM)
    anywhere = pl.BlockSpec(memory_space=pl.ANY)
    piece_shape = jax.ShapeDtypeStruct((rows, values), jnp.bfloat16)

    steps = [0] + inward(patches)
    mark = jax.ShapeDtypeStruct((8, 128), jnp.float32)
    *pieces, token = pl.pallas_call(
        functools.partial(split_kernel, steps),
        out_shape=[piece_shape] * patches + [mark],
        in_specs=[smem, vmem()],
        out_specs=[vmem()] * (patches + 1),
        compiler_params=params(),
        cost_estimate=cost(2 * 256 * rows * patches * values, 4 * rows * patches * values),
        name="split",
    )(me, ensemble.reshape(rows * patches, values))
    arrived = {k: ppermute(piece, "member", k) for k, piece in zip(steps, pieces)}
    store, token = lax.optimization_barrier((store, token))
    odd, even = swap(store, 1), swap(store, 0)

    table = jnp.concatenate([block_ids.ravel(), block_src.ravel(), block_count.ravel()])
    gram = pl.pallas_call(
        functools.partial(gram_kernel, 1.0 / (2.0 * size)),
        out_shape=jax.ShapeDtypeStruct((size, size), jnp.bfloat16),
        in_specs=[smem] * 2 + [anywhere] * 3,
        out_specs=vmem(),
        scratch_shapes=[
            pltpu.VMEM((slots * store.shape[1], size), jnp.bfloat16),
            pltpu.SemaphoreType.DMA((slots,)),
        ],
        compiler_params=params(),
        cost_estimate=cost(2 * slots * store.shape[1] * size * size, 4 * size * size),
        name="gram",
    )(region, table, store, even, odd)

    early = [k for k in steps if k and not is_late(k, patches)]
    late = [k for k in steps if is_late(k, patches)]
    matrix = jax.ShapeDtypeStruct((size, values), jnp.bfloat16)
    count = patches // PARTS + 1
    first_steps, early = early[:count], early + [0]
    token = pl.pallas_call(
        ahead_kernel,
        out_shape=mark,
        in_specs=[vmem()] + [anywhere] * count,
        out_specs=vmem(),
        compiler_params=params(),
        cost_estimate=cost(WEIGHT * size * size * values, 4 * count * rows * values),
        name="ahead",
    )(token, *[arrived[k] for k in first_steps])
    acc, members = pl.pallas_call(
        functools.partial(early_kernel, early),
        out_shape=[jax.ShapeDtypeStruct((size, values), jnp.float32), matrix],
        in_specs=[smem, vmem(), anywhere] + [vmem()] * len(early),
        out_specs=[vmem()] * 2,
        compiler_params=params(),
        cost_estimate=cost(1, 1),
        name="early",
    )(me, gram, token, *[arrived[k] for k in early])
    back = partners(patches) + [0]
    moved = pl.pallas_call(
        functools.partial(late_kernel, late, back),
        out_shape=[piece_shape] * patches,
        in_specs=[smem] + [vmem()] * (3 + len(late)),
        out_specs=[vmem()] * patches,
        scratch_shapes=[
            pltpu.VMEM((size, values), jnp.bfloat16),
            pltpu.VMEM((size // PARTS, values), jnp.bfloat16),
            pltpu.VMEM((size // 4, values), jnp.float32),
        ],
        compiler_params=params(),
        cost_estimate=cost(3 * size * size * values, 2 * size * size + 10 * size * values),
        name="late",
    )(me, *[arrived[k] for k in late], gram, acc, members)
    order = back
    returned = [ppermute(piece, "member", k) for k, piece in zip(back, moved)]

    steps = rows // rows_per_group(rows, patches)
    fresh = pl.pallas_call(
        functools.partial(merge_kernel, order),
        out_shape=jax.ShapeDtypeStruct((rows * patches, values), jnp.bfloat16),
        in_specs=[smem] + [vmem()] * patches,
        out_specs=pl.BlockSpec(memory_space=pl.ANY),
        scratch_shapes=[
            pltpu.VMEM((rows * patches, values), jnp.bfloat16),
            pltpu.SemaphoreType.DMA((steps,)),
        ],
        compiler_params=params(),
        cost_estimate=cost(2 * 256 * rows * patches * values, 4 * rows * patches * values),
        name="merge",
    )(me, *returned)
    return fresh.reshape(ensemble.shape)


def solution(mesh):
    return jax.shard_map(
        shards,
        mesh=mesh,
        in_specs=(
            P("member", "region", None, None),
            P("region", "member", None, None, None),
            P("region", "member", None),
            P("region", "member", None),
            P("region", "member"),
        ),
        out_specs=P("member", "region", None, None),
        check_vma=False,
    )
```

```python
import functools

import jax
import jax.numpy as jnp
from jax import lax
from jax.experimental import pallas as pl
from jax.experimental.pallas import tpu as pltpu
from jax.sharding import PartitionSpec as P

LIMIT = 16 * 1024 * 1024


def rows_per_group(rows, patches):
    return min(rows, max(16, 256 // patches))


PARTS = 4
WEIGHT = 40


def is_late(k, count):
    return k // (count // PARTS) == PARTS // 2


def outward(count):
    far = list(range(count - 1, count // 2 - 1, -1))
    near = list(range(count // 2 - 1, 0, -1))
    return far[:1] + near[:1] + far[1:] + near[1:]


def inward(count):
    quarter = count // PARTS
    return (
        list(range(count - 1, 3 * quarter - 1, -1))
        + list(range(2 * quarter - 1, 0, -1))
        + list(range(3 * quarter - 1, 2 * quarter - 1, -1))
    )


def ppermute(value, axis, step):
    if step == 0:
        return value
    count = lax.axis_size(axis)
    return lax.ppermute(value, axis, [(i, i ^ step) for i in range(count)])


def split_kernel(steps, me_ref, members_ref, *out_refs):
    patches = len(steps)
    rows = out_refs[0].shape[0]
    group = rows_per_group(rows, patches)
    height = group * patches
    row = lax.broadcasted_iota(jnp.int32, (height, height), 0)
    column = lax.broadcasted_iota(jnp.int32, (height, height), 1)
    source = lax.rem(row, group) * patches + (lax.div(row, group) ^ me_ref[0])
    shuffle = jnp.where(column == source, 1.0, 0.0).astype(jnp.bfloat16)
    for step in range(rows // group):
        block = members_ref[step * height : (step + 1) * height, :]
        moved = jnp.dot(shuffle, block, preferred_element_type=jnp.float32)
        moved = moved.astype(jnp.bfloat16)
        for k, out_ref in zip(steps, out_refs):
            out_ref[step * group : (step + 1) * group, :] = moved[k * group : (k + 1) * group, :]


def merge_kernel(order, me_ref, *refs):
    patches = len(order)
    piece_refs, (out_ref, whole, sem) = dict(zip(order, refs)), refs[patches:]
    rows = piece_refs[0].shape[0]
    group = rows_per_group(rows, patches)
    height = group * patches
    row = lax.broadcasted_iota(jnp.int32, (height, height), 0)
    column = lax.broadcasted_iota(jnp.int32, (height, height), 1)
    source = (lax.rem(row, patches) ^ me_ref[0]) * group + lax.div(row, patches)
    shuffle = jnp.where(column == source, 1.0, 0.0).astype(jnp.bfloat16)
    copies = []
    for step in range(rows // group):
        here = slice(step * group, (step + 1) * group)
        block = jnp.concatenate([piece_refs[k][here, :] for k in range(patches)], axis=0)
        moved = jnp.dot(shuffle, block, preferred_element_type=jnp.float32)
        there = pl.ds(step * height, height)
        whole[there, :] = moved.astype(jnp.bfloat16)
        copies.append(pltpu.make_async_copy(whole.at[there, :], out_ref.at[there, :], sem.at[step]))
        copies[-1].start()
    for copy in copies:
        copy.wait()


def gram_kernel(scale, region_ref, table_ref, own, even, odd, gram_ref, stacked, sem):
    slots = (table_ref.shape[0] - 1) // 2
    rows = own.shape[1]
    parity = lax.rem(region_ref[0], 2)
    count = table_ref[2 * slots]
    for slot in range(slots):
        live = slot < count
        target = stacked.at[pl.ds(slot * rows, rows), :]
        index, source = table_ref[slot], table_ref[slots + slot]
        where = jnp.where(source == 1, 0, jnp.where((source == 2) == (parity == 0), 1, 2))
        for code, store in enumerate((own, even, odd)):

            @pl.when(live & (where == code))
            def _():
                pltpu.make_async_copy(store.at[index], target, sem.at[slot]).start()

        @pl.when(jnp.logical_not(live))
        def _():
            target[...] = jnp.zeros(target.shape, target.dtype)

    for slot in range(slots):

        @pl.when(slot < count)
        def _():
            target = stacked.at[pl.ds(slot * rows, rows), :]
            pltpu.make_async_copy(odd.at[0], target, sem.at[slot]).wait()

    size = gram_ref.shape[0]
    part = min(size, 256)
    for step in range(size // part):
        block = lax.dot_general(
            stacked[:, step * part : (step + 1) * part],
            stacked[...],
            (((0,), (0,)), ((), ())),
            preferred_element_type=jnp.float32,
        )
        gram_ref[step * part : (step + 1) * part, :] = (block * scale).astype(jnp.bfloat16)


def block(me_ref, j, width, rows):
    return pl.ds(pl.multiple_of((lax.div(me_ref[0], width) ^ j) * rows, rows), rows)


def within(me_ref, k, quarter, rows):
    return pl.ds(pl.multiple_of(lax.rem(me_ref[0] ^ k, quarter) * rows, rows), rows)


def ahead_kernel(*refs):
    out_ref = refs[-1]
    for i, piece in enumerate(refs[:-1]):
        out_ref[i] = piece[...]


def early_kernel(steps, me_ref, gram_ref, ahead_ref, *refs):
    piece_refs, (acc_ref, members_ref) = refs[:-2], refs[-2:]
    rows = piece_refs[0].shape[0]
    piece_refs = [ahead_ref.at[i] for i in range(ahead_ref.shape[0])] + list(piece_refs)
    size = gram_ref.shape[0]
    there = block(me_ref, PARTS // 2, size // rows // PARTS, size // PARTS)
    members_ref[there, :] = jnp.zeros((size // PARTS, members_ref.shape[1]), members_ref.dtype)
    for k, piece in zip(steps, piece_refs):
        members_ref[pl.ds(pl.multiple_of((me_ref[0] ^ k) * rows, rows), rows), :] = piece[...]
    tall = size // 4
    for step in range(4):
        here = slice(step * tall, (step + 1) * tall)
        acc_ref[here, :] = jnp.dot(
            gram_ref[here, :], members_ref[...], preferred_element_type=jnp.float32
        )


def late_kernel(late_steps, out_steps, me_ref, *refs):
    count = len(late_steps)
    late_refs, outs = refs[:count], dict(zip(out_steps, refs[count + 3 : -3]))
    gram_ref, acc_ref, members_ref = refs[count : count + 3]
    first, late, fresh = refs[-3:]
    rows = late_refs[0].shape[0]
    size = gram_ref.shape[0]
    width = late.shape[0] // rows
    for k, piece in zip(late_steps, late_refs):
        late[within(me_ref, k, width, rows), :] = piece[...]
    there = block(me_ref, PARTS // 2, width, late.shape[0])
    tall = size // 4
    for step in range(4):
        here = slice(step * tall, (step + 1) * tall)
        part = jnp.dot(gram_ref[here, there], late[...], preferred_element_type=jnp.float32)
        first[here, :] = (acc_ref[here, :] + part).astype(jnp.bfloat16)
    quarter = tall // rows
    for j in (3, 2, 1, 0):
        there = block(me_ref, j, quarter, tall)
        second = jnp.dot(gram_ref[there, :], first[...], preferred_element_type=jnp.float32)
        rest = members_ref[there, :].astype(jnp.float32) - first[there, :].astype(jnp.float32)
        fresh[...] = rest + second
        for k in late_steps:
            if k // quarter == j:
                here = within(me_ref, k, quarter, rows)
                fresh[here, :] += late[within(me_ref, k, width, rows), :].astype(jnp.float32)
        for k, out_ref in outs.items():
            if k // quarter == j:
                here = within(me_ref, k, quarter, rows)
                out_ref[...] = fresh[here, :].astype(jnp.bfloat16)


def vmem():
    return pl.BlockSpec(memory_space=pltpu.VMEM)


def params():
    return pltpu.CompilerParams(vmem_limit_bytes=LIMIT)


def cost(flops, nbytes):
    return pl.CostEstimate(flops=flops, bytes_accessed=nbytes, transcendentals=0)


def swap(store, first):
    count = lax.axis_size("region")
    pairs = [(i, i + 1) for i in range(first, count - 1, 2)]
    return lax.ppermute(store, "region", pairs + [(j, i) for i, j in pairs])


def shards(ensemble, obs_store, block_ids, block_src, block_count):
    rows, _, patches, values = ensemble.shape
    store = obs_store.reshape(obs_store.shape[2:])
    size = store.shape[2]
    slots = block_ids.shape[2]
    me = lax.axis_index("member").astype(jnp.int32).reshape(1)
    region = lax.axis_index("region").astype(jnp.int32).reshape(1)
    smem = pl.BlockSpec(memory_space=pltpu.SMEM)
    hbm = pl.BlockSpec(memory_space=pltpu.HBM)
    piece_shape = jax.ShapeDtypeStruct((rows, values), jnp.bfloat16)

    steps = [0] + inward(patches)
    pieces = pl.pallas_call(
        functools.partial(split_kernel, steps),
        out_shape=[piece_shape] * patches,
        in_specs=[smem, vmem()],
        out_specs=[vmem()] * patches,
        compiler_params=params(),
        cost_estimate=cost(2 * 256 * rows * patches * values, 4 * rows * patches * values),
        name="split",
    )(me, ensemble.reshape(rows * patches, values))
    arrived = {k: ppermute(piece, "member", k) for k, piece in zip(steps, pieces)}
    store, _ = lax.optimization_barrier((store, pieces[0]))
    odd, even = swap(store, 1), swap(store, 0)

    table = jnp.concatenate([block_ids.ravel(), block_src.ravel(), block_count.ravel()])
    gram = pl.pallas_call(
        functools.partial(gram_kernel, 1.0 / (2.0 * size)),
        out_shape=jax.ShapeDtypeStruct((size, size), jnp.bfloat16),
        in_specs=[smem] * 2 + [hbm] * 3,
        out_specs=vmem(),
        scratch_shapes=[
            pltpu.VMEM((slots * store.shape[1], size), jnp.bfloat16),
            pltpu.SemaphoreType.DMA((slots,)),
        ],
        compiler_params=params(),
        cost_estimate=cost(2 * slots * store.shape[1] * size * size, 4 * size * size),
        name="gram",
    )(region, table, store, even, odd)

    early = [k for k in steps if k and not is_late(k, patches)]
    late = [k for k in steps if is_late(k, patches)]
    matrix = jax.ShapeDtypeStruct((size, values), jnp.bfloat16)
    count = patches // PARTS + 1
    first_steps, early = early[:count], early[count:] + [0]
    ahead = pl.pallas_call(
        ahead_kernel,
        out_shape=jax.ShapeDtypeStruct((count, rows, values), jnp.bfloat16),
        in_specs=[vmem()] * count,
        out_specs=vmem(),
        compiler_params=params(),
        cost_estimate=cost(WEIGHT * size * size * values, 4 * count * rows * values),
        name="ahead",
    )(*[arrived[k] for k in first_steps])
    acc, members = pl.pallas_call(
        functools.partial(early_kernel, first_steps + early),
        out_shape=[jax.ShapeDtypeStruct((size, values), jnp.float32), matrix],
        in_specs=[smem] + [vmem()] * (2 + len(early)),
        out_specs=[vmem()] * 2,
        compiler_params=params(),
        cost_estimate=cost(1, 1),
        name="early",
    )(me, gram, ahead, *[arrived[k] for k in early])
    back = outward(patches) + [0]
    moved = pl.pallas_call(
        functools.partial(late_kernel, late, back),
        out_shape=[piece_shape] * patches,
        in_specs=[smem] + [vmem()] * (3 + len(late)),
        out_specs=[vmem()] * patches,
        scratch_shapes=[
            pltpu.VMEM((size, values), jnp.bfloat16),
            pltpu.VMEM((size // PARTS, values), jnp.bfloat16),
            pltpu.VMEM((size // 4, values), jnp.float32),
        ],
        compiler_params=params(),
        cost_estimate=cost(3 * size * size * values, 2 * size * size + 10 * size * values),
        name="late",
    )(me, *[arrived[k] for k in late], gram, acc, members)
    order = back
    returned = [ppermute(piece, "member", k) for k, piece in zip(back, moved)]

    steps = rows // rows_per_group(rows, patches)
    fresh = pl.pallas_call(
        functools.partial(merge_kernel, order),
        out_shape=jax.ShapeDtypeStruct((rows * patches, values), jnp.bfloat16),
        in_specs=[smem] + [vmem()] * patches,
        out_specs=pl.BlockSpec(memory_space=pl.ANY),
        scratch_shapes=[
            pltpu.VMEM((rows * patches, values), jnp.bfloat16),
            pltpu.SemaphoreType.DMA((steps,)),
        ],
        compiler_params=params(),
        cost_estimate=cost(2 * 256 * rows * patches * values, 4 * rows * patches * values),
        name="merge",
    )(me, *returned)
    return fresh.reshape(ensemble.shape)


def solution(mesh):
    return jax.shard_map(
        shards,
        mesh=mesh,
        in_specs=(
            P("member", "region", None, None),
            P("region", "member", None, None, None),
            P("region", "member", None),
            P("region", "member", None),
            P("region", "member"),
        ),
        out_specs=P("member", "region", None, None),
        check_vma=False,
    )
```
